32 devices in a mesh: mem: 8 (over y, x, core), cell: 4 (over z).
Axes of the slice: x: 2, y: 2, z: 4, core: 2. Of those that a mesh axis runs over, the one named last changes fastest.
Arguments:
- prior_ensemble: bfloat16 [512, 2, 32768], P('mem', None, 'cell'), may hold values from -12 to 12
- measurement_location: int32 [16, 1024], P('cell', 'mem'), may hold values from 0 to 65535, as said below
- measurement_datum: float32 [16, 1024], P('cell', 'mem'), may hold values from -32 to 32
- measurement_spread: float32 [16, 1024], P('cell', 'mem'), may hold values from 1.2 to 20
Outputs:
- analysis: bfloat16 [512, 2, 32768], P('mem', None, 'cell')
The draws below stay inside these ranges and needn't reach their ends.
Inputs may be any that keep to these rules, and one draw needn't show every extreme that they name: `measurement_location`: with v an entry at row r and column c, v // 32768 is its field and v % 32768 its cell; that cell is one of the 1024 cells that begin at ((r // 4) * 8 + c // 128) * 1024. Within each such block of 4 rows and 128 columns the entries are distinct, and they include the first cell of field 0 and the last cell of field 1 of that range.
All inputs are finite; a program needn't handle non-finite values.
Results may differ from the reference program's by a relative error of at most 0.0063.
Values may be sent and summed in bfloat16 or wider, within the bound.
A program may use at most 64 MiB of HBM per device.

```python
import math
import jax
import jax.numpy as jnp
from jax import lax

M = 512
GRID_SHARE_SPAN = 1024
OBS_ROWS = 4
NS_ITERS = 8
CELLS = 32768
OBS_R = 16
OBS_C = 1024
N_MEM = 8
N_CELL = 4


def draw_prior_ensemble(key, part):
    keys = jax.random.split(key, 7)
    pattern_count = 24
    base = jax.random.normal(keys[0], (1, 2, CELLS), jnp.float32)
    cell_scale = jnp.exp(jax.random.uniform(keys[1], (1, 2, CELLS), jnp.float32, math.log(0.5), math.log(2.0)))
    patterns = jax.random.normal(keys[2], (pattern_count, 2, CELLS), jnp.float32)
    strength = jnp.exp(jax.random.uniform(keys[3], (pattern_count,), jnp.float32, math.log(0.06), math.log(0.25)))
    member_scale = jnp.exp(jax.random.uniform(keys[5], (M, 1, 1), jnp.float32, math.log(0.15), math.log(0.6)))
    coefs = jax.random.normal(keys[4], (M, pattern_count), jnp.float32)
    noise = jax.random.normal(keys[6], (M, 2, CELLS), jnp.float32)
    signal = member_scale * noise
    for index in range(pattern_count):
        signal = signal + (coefs[:, index] * strength[index])[:, None, None] * patterns[index][None, :, :]
    return jnp.clip(base + cell_scale * signal, -12.0, 12.0).astype(jnp.bfloat16)


def draw_measurement_location(key, part):
    block_count = N_MEM * N_CELL
    obs_dev = OBS_ROWS * 128
    keys = jax.random.split(jax.random.fold_in(key, 17), block_count)

    def one_block(block_key):
        key_inner, key_order = jax.random.split(block_key)
        inner = jax.random.permutation(key_inner, 2 * GRID_SHARE_SPAN - 2)[:obs_dev - 2].astype(jnp.int32) + 1
        chosen = jnp.concatenate([jnp.array([0, 2 * GRID_SHARE_SPAN - 1], jnp.int32), inner])
        return jax.random.permutation(key_order, chosen)
    slot_table = jax.vmap(one_block)(keys)
    block_id = jnp.arange(block_count, dtype=jnp.int32)[:, None]
    cell_ids = slot_table // GRID_SHARE_SPAN * CELLS + block_id * GRID_SHARE_SPAN + slot_table % GRID_SHARE_SPAN
    cell_ids = cell_ids.reshape(N_CELL, N_MEM, OBS_ROWS, 128).transpose(0, 2, 1, 3)
    return cell_ids.reshape(OBS_ROWS * N_CELL, 128 * N_MEM).astype(jnp.int32)


def draw_measurement_spread(key, part):
    keys = jax.random.split(jax.random.fold_in(key, 29), 2)
    block_count = N_MEM * N_CELL
    base = jnp.exp(jax.random.uniform(keys[0], (N_CELL, OBS_ROWS, N_MEM, 128), jnp.float32, math.log(4.0), math.log(20.0)))
    heavy_ids = jax.random.permutation(keys[1], block_count)[:2]
    block_ids = jnp.arange(block_count, dtype=jnp.int32)
    heavy = jnp.any(block_ids[:, None] == heavy_ids[None, :], axis=1)
    factor = jnp.where(heavy, 0.3, 1.0).astype(jnp.float32).reshape(N_CELL, 1, N_MEM, 1)
    return (base * factor).reshape(OBS_ROWS * N_CELL, 128 * N_MEM).astype(jnp.float32)


def steps_of(rng, extent, shards, low, largest):
    gain, own = 1.0, jax.random.fold_in(rng, 6)
    for dim, shards_of in shards:
        steps = jnp.exp(jax.random.uniform(jax.random.fold_in(own, dim), (shards_of,), jnp.float32, low / len(shards), largest / len(shards)))
        gain = gain * jnp.repeat(steps, extent[dim] // shards_of).reshape([-1 if axis == dim else 1 for axis in range(len(extent))])
    return gain


def normal_values(rng, shape, scale, reach, pieces=(), held_as=jnp.bfloat16):
    values = scale * jax.random.normal(rng, shape, jnp.float32)
    if pieces:
        values = values * steps_of(rng, shape, pieces, -0.22, 0.18)
    return jnp.clip(values, -reach, reach).astype(held_as)


def setup_inputs(seed: int = 0) -> dict:
    streams_of = jax.random.split(jax.random.key(seed), 5)
    return {
        "prior_ensemble": draw_prior_ensemble(jax.random.fold_in(streams_of[4], 71), 0),
        "measurement_location": draw_measurement_location(jax.random.fold_in(streams_of[4], 71), 0),
        "measurement_datum": normal_values(streams_of[2], (OBS_R, OBS_C), 8.0, 32.0, ((0, 4), (1, 8)), jnp.float32),
        "measurement_spread": draw_measurement_spread(jax.random.fold_in(streams_of[4], 71), 0),
    }


def reference(prior_ensemble, measurement_location, measurement_datum, measurement_spread):
    ensemble_size = prior_ensemble.shape[0]
    grid_site_number = prior_ensemble.shape[2]
    norm_factor = math.sqrt(ensemble_size - 1)
    highest = lax.Precision.HIGHEST
    cell_ids = measurement_location.reshape(-1)
    values = measurement_datum.reshape(-1)
    errors = measurement_spread.reshape(-1)
    group_size = OBS_ROWS * 128
    groups = cell_ids.shape[0] // group_size

    def add_group(group_index, totals):
        gram_sum, projected = totals
        first_obs = (group_index * group_size).astype(jnp.int32)
        label_fraction = lax.dynamic_slice_in_dim(cell_ids, first_obs, group_size)
        err_part = lax.dynamic_slice_in_dim(errors, first_obs, group_size)
        val_part = lax.dynamic_slice_in_dim(values, first_obs, group_size)
        picked_lines = prior_ensemble[:, label_fraction // grid_site_number, label_fraction % grid_site_number].astype(jnp.float32)
        mean_obs = lax.optimization_barrier(jnp.mean(picked_lines, axis=0))
        anomaly = (picked_lines - mean_obs).astype(jnp.bfloat16)
        scaled = (anomaly.astype(jnp.float32) / (err_part * norm_factor)).astype(jnp.bfloat16)
        innovation = ((val_part - mean_obs) / err_part).astype(jnp.bfloat16)
        scaled_wide = scaled.astype(jnp.float32)
        gram_sum = gram_sum + lax.dot_general(scaled_wide, scaled_wide, (((1,), (1,)), ((), ())), precision=highest)
        projected = projected + jnp.dot(scaled_wide, innovation.astype(jnp.float32), precision=highest)
        return (gram_sum, projected)
    start_totals = (jnp.zeros((ensemble_size, ensemble_size), jnp.float32), jnp.zeros((ensemble_size,), jnp.float32))
    gram_sum, projected = lax.fori_loop(0, groups, add_group, start_totals)
    identity = jnp.eye(ensemble_size, dtype=jnp.float32)
    system = gram_sum + identity
    norm_scale = jnp.sqrt(jnp.sum(system * system))

    def newton_turn(turn, pair):
        iterate_y, iterate_z = pair
        newton_step = 1.5 * identity - 0.5 * jnp.dot(iterate_z, iterate_y, precision=highest)
        return (jnp.dot(newton_step, iterate_y, precision=highest), jnp.dot(newton_step, iterate_z, precision=highest))
    iterate_y, iterate_z = lax.fori_loop(0, NS_ITERS, newton_turn, (system / norm_scale, identity))
    shift_weights = jnp.dot(iterate_z, projected, precision=highest) / (jnp.sqrt(norm_scale) * norm_factor)
    weights = (iterate_z / jnp.sqrt(norm_scale)).astype(jnp.bfloat16).astype(jnp.float32)
    tile_sequence = grid_site_number // GRID_SHARE_SPAN

    def renew_tile(block_index, analysis):
        initial_grid_site = (block_index * GRID_SHARE_SPAN).astype(jnp.int32)
        tile_fraction = lax.dynamic_slice_in_dim(prior_ensemble, initial_grid_site, GRID_SHARE_SPAN, 2)
        flat_state = tile_fraction.reshape(ensemble_size, 2 * GRID_SHARE_SPAN).astype(jnp.float32)
        mean_state = lax.optimization_barrier(jnp.mean(flat_state, axis=0))
        anomalies = (flat_state - mean_state).astype(jnp.bfloat16).astype(jnp.float32)
        updated = jnp.dot(weights, anomalies, precision=highest)
        mean_shift = jnp.dot(shift_weights, updated, precision=highest)
        block_out = (mean_state + mean_shift + updated).astype(jnp.bfloat16).reshape(ensemble_size, 2, GRID_SHARE_SPAN)
        return lax.dynamic_update_slice_in_dim(analysis, block_out, initial_grid_site, 2)
    return lax.fori_loop(0, tile_sequence, renew_tile, jnp.zeros(prior_ensemble.shape, jnp.bfloat16))
```

```python
import functools
import math

import jax
import jax.numpy as jnp
from jax import lax
from jax.experimental import pallas as pl
from jax.experimental.pallas import tpu as pltpu
from jax.sharding import PartitionSpec as P

NS_ITERS = 8
LANES = 128
BF, F32 = jnp.bfloat16, jnp.float32
MESH = pl.DeviceIdType.MESH


def iota(shape, dim):
    return lax.broadcasted_iota(jnp.int32, shape, dim)


def remote(src, dst, send, recv, where):
    return pltpu.make_async_remote_copy(
        src_ref=src, dst_ref=dst, send_sem=send, recv_sem=recv, device_id=where, device_id_type=MESH
    )


def nt(a, b):
    return lax.dot_general(a, b, (((1,), (1,)), ((), ())), preferred_element_type=F32)


def nn(a, b):
    return jnp.dot(a, b, preferred_element_type=F32)


def thirds(v):
    hi = v.astype(BF)
    rest = v - hi.astype(F32)
    mid = rest.astype(BF)
    lo = (rest - mid.astype(F32)).astype(BF)
    return hi, mid, lo


def row_times(v, mat):
    parts = thirds(v)
    row = iota((16, v.shape[1]), 0)
    stack = jnp.zeros((16, v.shape[1]), F32)
    for i, part in enumerate(parts):
        stack = jnp.where(row == i, part.astype(F32), stack)
    return jnp.sum(nn(stack.astype(BF), mat), axis=0, keepdims=True)


def kernel(
    dims, x, loc, datum, spread, y,
    held, anom, means, hot, scaled, gram, r1, s1, r2, s2, r3, full,
    sys_f, u_f, z_f, his, los, wts, base, outs,
    a_send, a_recv, own_sem, c_send, c_recv, q_send, q_recv, z_send, z_recv,
    zg_send, zg_recv, qg_send, qg_recv, cg_send, cg_recv, o_send, o_recv,
):
    n, nz, members, fields, cells, mloc, grid_cells = dims
    rows = mloc * fields
    nq = n // 2
    total = gram.shape[0]
    half, quart = total // 2, total // 2 // nq
    piece = quart // nz
    norm_factor = math.sqrt(members - 1)
    me, mz = lax.axis_index("mem"), lax.axis_index("cell")
    core, chip = lax.rem(me, 2), lax.div(me, 2)
    mate = me + 1 - 2 * core

    barrier = pltpu.get_barrier_semaphore()
    for d in range(1, n):
        pl.semaphore_signal(barrier, inc=1, device_id={"mem": lax.rem(me + d, n)}, device_id_type=MESH)
    for d in range(1, nz):
        pl.semaphore_signal(barrier, inc=1, device_id={"cell": lax.rem(mz + d, nz)}, device_id_type=MESH)
    pl.semaphore_wait(barrier, n - 1 + nz - 1)

    def col(p):
        return pl.ds(pl.multiple_of(p * cells, cells), cells)

    def block(p):
        return pl.ds(pl.multiple_of(p * rows, rows), rows)

    def share(p):
        return pl.ds(pl.multiple_of(p * mloc, mloc), mloc)

    def send_in(d, _):
        p = lax.rem(me + d, n)
        remote(x.at[:, col(p)], held.at[block(me)], a_send.at[d], a_recv.at[d], {"mem": p}).start()
        return 0

    lax.fori_loop(1, n, send_in, 0)
    own = pltpu.make_async_copy(x.at[:, col(me)], held.at[block(me)], own_sem)
    own.start()

    first_cell = (mz * n + me) * cells
    obs_rows = loc.shape[0]
    obs = obs_rows * LANES
    v = loc[...]
    slots = v - first_cell
    for f in range(1, fields):
        slots = slots + jnp.where(v >= f * grid_cells, cells - grid_cells, 0)

    def build(i, _):
        at = pl.ds(pl.multiple_of(i * LANES, LANES), LANES)
        cell = iota((LANES, LANES), 0) + i * LANES
        for r in range(obs_rows):
            hot[at, r * LANES:(r + 1) * LANES] = jnp.where(cell == slots[r:r + 1, :], 1.0, 0.0).astype(BF)
        return 0

    lax.fori_loop(0, fields * cells // LANES, build, 0)

    means[...] = jnp.zeros_like(means)

    def take(p):
        got = held[block(p), :]
        for f in range(fields):
            pick = jnp.where(iota((mloc, rows), 1) == iota((mloc, rows), 0) * fields + f, 1.0, 0.0).astype(BF)
            lines = nn(pick, got)
            at = slice(f * cells, (f + 1) * cells)
            anom[share(p), at] = lines.astype(BF)
            means[:, at] += jnp.sum(lines, axis=0, keepdims=True)

    own.wait()
    take(me)

    def arrive(d, _):
        p = lax.rem(me + n - d, n)
        remote(x.at[:, col(p)], held.at[block(p)], a_send.at[d], a_recv.at[d], {"mem": p}).wait_recv()
        take(p)
        return 0

    lax.fori_loop(1, n, arrive, 0)
    means[...] = means[...] / members

    def centre(i, _):
        at = pl.ds(pl.multiple_of(i * 64, 64), 64)
        lines = (anom[at, :].astype(F32) - means[...]).astype(BF)
        anom[at, :] = lines
        return 0

    lax.fori_loop(0, members // 64, centre, 0)

    errors = jnp.concatenate([spread[r:r + 1, :] for r in range(obs_rows)], axis=1)
    values = jnp.concatenate([datum[r:r + 1, :] for r in range(obs_rows)], axis=1)
    inverse = 1.0 / (errors * norm_factor)
    mean_obs = row_times(means[...], hot[...])
    innovation = ((values - mean_obs) / errors).astype(BF)

    def pick_rows(i, _):
        at = pl.ds(pl.multiple_of(i * 256, 256), 256)
        scaled[at, :] = (nn(anom[at, :], hot[...]) * inverse).astype(BF)
        return 0

    lax.fori_loop(0, members // 256, pick_rows, 0)
    spread16 = jnp.where(iota((16, obs), 0) == 0, innovation.astype(F32), 0.0).astype(BF)
    projected = jnp.sum(nt(spread16, scaled[...]), axis=0, keepdims=True)

    nb = members // LANES
    lane, line = iota((LANES, LANES), 1), iota((LANES, LANES), 0)
    place = 0
    for bi in range(nb):
        strip = nt(scaled[bi * LANES:(bi + 1) * LANES, :], scaled[bi * LANES:, :])
        for bj in range(bi, nb):
            blk = strip[:, (bj - bi) * LANES:(bj - bi + 1) * LANES]
            if bi == bj:
                chunk = projected[:, bi * LANES:(bi + 1) * LANES]
                turned = pltpu.roll(jnp.broadcast_to(chunk, (8, LANES)), LANES // 2, 1)[0:1, :]
                low = lane < LANES // 2
                blk = jnp.where(low & (line == LANES - 1), chunk, blk)
                blk = jnp.where(low & (line == LANES - 2), turned, blk)
            gram[place * LANES:(place + 1) * LANES, :] = blk
            place += 1
    if place * LANES < total:
        gram[place * LANES:, :] = jnp.zeros((total - place * LANES, LANES), F32)

    def cut(start, size):
        return pl.ds(pl.multiple_of(start, 8), size)

    go = remote(gram.at[cut((1 - core) * half, half)], r1, c_send, c_recv, {"mem": mate})
    go.start()
    go.wait_recv()
    s1[...] = gram[cut(core * half, half), :] + r1[...]

    def to_chip(d):
        return lax.rem(lax.rem(chip + d, nq) * 2 + core, n)

    def plane(d):
        q = lax.rem(chip + d, nq)
        return remote(s1.at[cut(q * quart, quart)], r2.at[d], q_send.at[d], q_recv.at[d], {"mem": to_chip(d)})

    for d in range(1, nq):
        plane(d).start()
    acc = s1[cut(chip * quart, quart), :]
    for d in range(1, nq):
        plane(d).wait_recv()
        acc = acc + r2[d]
    s2[...] = acc

    def line_of(d):
        k = lax.rem(mz + d, nz)
        return remote(s2.at[cut(k * piece, piece)], r3.at[d], z_send.at[d], z_recv.at[d], {"cell": k})

    for d in range(1, nz):
        line_of(d).start()
    acc = s2[cut(mz * piece, piece), :]
    for d in range(1, nz):
        line_of(d).wait_recv()
        acc = acc + r3[d]
    mine = core * half + chip * quart
    full[cut(mine + mz * piece, piece), :] = acc

    def line_back(d, k):
        at = full.at[cut(mine + k * piece, piece)]
        return remote(at, at, zg_send.at[d], zg_recv.at[d], {"cell": lax.rem(mz + d, nz)})

    for d in range(1, nz):
        line_back(d, mz).start()
    for d in range(1, nz):
        line_back(d, lax.rem(mz + nz - d, nz)).wait_recv()

    def plane_back(d, q):
        at = full.at[cut(core * half + q * quart, quart)]
        return remote(at, at, qg_send.at[d], qg_recv.at[d], {"mem": to_chip(d)})

    def pair_back(d, c, q):
        at = full.at[cut(c * half + q * quart, quart)]
        return remote(at, at, cg_send.at[d], cg_recv.at[d], {"mem": mate})

    for d in range(1, nq):
        plane_back(d, chip).start()
    pair_back(0, core, chip).start()
    for d in range(1, nq):
        q = lax.rem(chip + nq - d, nq)
        plane_back(d, q).wait_recv()
        pair_back(d, core, q).start()
    for d in range(nq):
        pair_back(d, 1 - core, lax.rem(chip + nq - d, nq)).wait_recv()

    place = 0
    squares = jnp.zeros((1, LANES), F32)
    proj = []
    for bi in range(nb):
        for bj in range(bi, nb):
            blk = full[place * LANES:(place + 1) * LANES, :]
            place += 1
            here, there = slice(bi * LANES, (bi + 1) * LANES), slice(bj * LANES, (bj + 1) * LANES)
            if bi == bj:
                first, second = blk[LANES - 1:, :], blk[LANES - 2:LANES - 1, :]
                second = pltpu.roll(jnp.broadcast_to(second, (8, LANES)), LANES // 2, 1)[0:1, :]
                proj.append(jnp.where(iota((1, LANES), 1) < LANES // 2, first, second))
                blk = jnp.where(lane >= line, blk, blk.T) + jnp.where(lane == line, 1.0, 0.0)
                sys_f[here, here] = blk
                squares = squares + jnp.sum(blk * blk, axis=0, keepdims=True)
            else:
                sys_f[here, there] = blk
                sys_f[there, here] = blk.T
                squares = squares + 2.0 * jnp.sum(blk * blk, axis=0, keepdims=True)
    projected = jnp.concatenate(proj, axis=1)
    norm_scale = jnp.sqrt(jnp.sum(squares, axis=1, keepdims=True))
    inv_norm = 1.0 / norm_scale

    IP, IU, IQ, IT, IZ = range(5)
    step = 256 if members % 256 == 0 else LANES
    chunks = members // step

    def keep(slot, at, val):
        hi = val.astype(BF)
        his[slot, at, :] = hi
        los[slot, at, :] = (val - hi.astype(F32)).astype(BF)

    def times(a, b, finish):
        def go(i, _):
            at = pl.ds(pl.multiple_of(i * step, step), step)
            ah, al = his[a, at, :], los[a, at, :]
            finish(at, i, nn(ah, his[b]) + nn(ah, los[b]) + nn(al, his[b]))
            return 0

        lax.fori_loop(0, chunks, go, 0)

    def scale(i, _):
        at = pl.ds(pl.multiple_of(i * 64, 64), 64)
        val = sys_f[at, :] * inv_norm
        sys_f[at, :] = val
        keep(IP, at, val)
        return 0

    lax.fori_loop(0, members // 64, scale, 0)

    def quartic(into):
        def first(at, i, val):
            val = val - 4.5 * sys_f[at, :]
            u_f[at, :] = val
            keep(IU, at, val)

        times(IP, IP, first)

        def second(at, i, val):
            val = 0.0625 * val + 0.421875 * u_f[at, :] - 0.5390625 * sys_f[at, :]
            diagonal = iota((step, members), 1) == iota((step, members), 0) + i * step
            val = val + jnp.where(diagonal, 2.25, 0.0)
            for slot in into:
                keep(slot, at, val)

        times(IU, IU, second)

    def renew():
        times(IQ, IP, lambda at, i, val: keep(IT, at, val))

        def last(at, i, val):
            sys_f[at, :] = val
            keep(IP, at, val)

        times(IQ, IT, last)

    quartic((IQ, IZ))
    renew()

    def pair_turn(turn, _):
        now = IZ + turn
        quartic((IQ,))
        times(IQ, now, lambda at, i, val: keep(now + 1, at, val))
        renew()
        return 0

    lax.fori_loop(0, NS_ITERS // 2 - 2, pair_turn, 0)
    quartic((IQ,))

    def final(at, i, val):
        z_f[at, :] = val

    times(IQ, IZ + NS_ITERS // 2 - 2, final)

    root = 1.0 / jnp.sqrt(norm_scale)

    def weigh(i, carry):
        at = pl.ds(pl.multiple_of(i * 64, 64), 64)
        val = z_f[at, :]
        w = (val * root).astype(BF)
        wts[at, :] = w
        shift = jnp.sum(val * projected, axis=1, keepdims=True) * (root * (1.0 / norm_factor))
        return carry + jnp.sum(shift * w.astype(F32), axis=0, keepdims=True)

    mixed = lax.fori_loop(0, members // 64, weigh, jnp.zeros((1, members), F32))
    base[...] = means[...] + row_times(mixed, anom[...])

    def make(p):
        double = jnp.where(
            (iota((rows, mloc), 0) >= iota((rows, mloc), 1) * fields)
            & (iota((rows, mloc), 0) < iota((rows, mloc), 1) * fields + fields), 1.0, 0.0).astype(BF)
        w2 = nn(double, wts[share(p), :]).astype(BF)
        field = iota((rows, cells), 0) & (fields - 1)
        out = None
        for f in range(fields):
            at = slice(f * cells, (f + 1) * cells)
            part = nn(w2, anom[:, at]) + base[:, at]
            out = part if out is None else jnp.where(field == f, part, out)
        return out.astype(BF)

    def out_copy(d, p, to):
        return remote(outs.at[p], y.at[:, col(to)], o_send.at[d], o_recv.at[d], {"mem": p})

    def send_out(d, _):
        p = lax.rem(me + d, n)
        outs[p] = make(p)
        out_copy(d, p, me).start()
        return 0

    lax.fori_loop(1, n, send_out, 0)
    outs[me] = make(me)
    own = pltpu.make_async_copy(outs.at[me], y.at[:, col(me)], own_sem)
    own.start()

    def finish_out(d, _):
        p = lax.rem(me + n - d, n)
        out_copy(d, p, p).wait_recv()
        return 0

    lax.fori_loop(1, n, finish_out, 0)
    own.wait()

    def sent(d, _):
        p = lax.rem(me + d, n)
        remote(x.at[:, col(p)], held.at[block(me)], a_send.at[d], a_recv.at[d], {"mem": p}).wait_send()
        out_copy(d, p, me).wait_send()
        return 0

    lax.fori_loop(1, n, sent, 0)
    go.wait_send()
    for d in range(1, nq):
        plane(d).wait_send()
        plane_back(d, chip).wait_send()
    for d in range(1, nz):
        line_of(d).wait_send()
        line_back(d, mz).wait_send()
    for d in range(nq):
        pair_back(d, core, lax.rem(chip + nq - d, nq)).wait_send()


def local(prior_ensemble, measurement_location, measurement_datum, measurement_spread):
    n, nz = lax.axis_size("mem"), lax.axis_size("cell")
    mloc, fields, width = prior_ensemble.shape
    members, cells, rows = mloc * n, width // n, mloc * fields
    obs = measurement_location.size
    nb = members // LANES
    unit = 8 * n * nz
    total = -(-(nb * (nb + 1) // 2 * LANES) // unit) * unit
    half, nq = total // 2, n // 2
    quart = half // nq
    piece = quart // nz
    dims = (n, nz, members, fields, cells, mloc, width * nz)
    zslots = 4 + NS_ITERS // 2 - 1
    vm, dma = pltpu.VMEM, pltpu.SemaphoreType.DMA
    square = (members, members)
    scratch = [
        vm((n * rows, cells), BF), vm((members, fields * cells), BF), vm((1, fields * cells), F32),
        vm((fields * cells, obs), BF), vm((members, obs), BF),
        vm((total, LANES), F32), vm((half, LANES), F32), vm((half, LANES), F32),
        vm((nq, quart, LANES), F32), vm((quart, LANES), F32), vm((nz, piece, LANES), F32),
        vm((total, LANES), F32),
        vm(square, F32), vm(square, F32), vm(square, F32),
        vm((zslots,) + square, BF), vm((zslots,) + square, BF), vm(square, BF),
        vm((1, fields * cells), F32), vm((n, rows, cells), BF),
        dma((n,)), dma((n,)), dma, dma, dma, dma((nq,)), dma((nq,)), dma((nz,)), dma((nz,)),
        dma((nz,)), dma((nz,)), dma((nq,)), dma((nq,)), dma((nq,)), dma((nq,)), dma((n,)), dma((n,)),
    ]
    out = pl.pallas_call(
        functools.partial(kernel, dims),
        out_shape=jax.ShapeDtypeStruct((rows, width), BF),
        in_specs=[pl.BlockSpec(memory_space=pl.ANY)] + [pl.BlockSpec(memory_space=pltpu.VMEM)] * 3,
        out_specs=pl.BlockSpec(memory_space=pl.ANY),
        scratch_shapes=scratch,
        compiler_params=pltpu.CompilerParams(
            collective_id=0, has_side_effects=True, vmem_limit_bytes=50 * 1024 * 1024
        ),
    )(prior_ensemble.reshape(rows, width), measurement_location, measurement_datum, measurement_spread)
    return out.reshape(mloc, fields, width)


def solution(mesh):
    placed = (P("mem", None, "cell"), P("cell", "mem"), P("cell", "mem"), P("cell", "mem"))
    return jax.shard_map(
        local, mesh=mesh, in_specs=placed, out_specs=P("mem", None, "cell"), check_vma=False
    )
```

```python
import functools
import math

import jax
import jax.numpy as jnp
from jax import lax
from jax.experimental import pallas as pl
from jax.experimental.pallas import tpu as pltpu
from jax.sharding import PartitionSpec as P

NS_ITERS = 8
LANES = 128
BF, F32 = jnp.bfloat16, jnp.float32
MESH = pl.DeviceIdType.MESH


def iota(shape, dim):
    return lax.broadcasted_iota(jnp.int32, shape, dim)


def remote(src, dst, send, recv, where):
    return pltpu.make_async_remote_copy(
        src_ref=src, dst_ref=dst, send_sem=send, recv_sem=recv, device_id=where, device_id_type=MESH
    )


def nt(a, b):
    return lax.dot_general(a, b, (((1,), (1,)), ((), ())), preferred_element_type=F32)


def nn(a, b):
    return jnp.dot(a, b, preferred_element_type=F32)


def thirds(v):
    hi = v.astype(BF)
    rest = v - hi.astype(F32)
    mid = rest.astype(BF)
    lo = (rest - mid.astype(F32)).astype(BF)
    return hi, mid, lo


def row_times(v, mat):
    parts = thirds(v)
    row = iota((16, v.shape[1]), 0)
    stack = jnp.zeros((16, v.shape[1]), F32)
    for i, part in enumerate(parts):
        stack = jnp.where(row == i, part.astype(F32), stack)
    return jnp.sum(nn(stack.astype(BF), mat), axis=0, keepdims=True)


def kernel(
    dims, x, loc, datum, spread, y,
    near, places, picked, raw, held, anom, means, hot, scaled, gram, r1, s1, r2, s2, r3, full,
    sys_f, u_f, z_f, his, los, wts, base, outs,
    near_sem, l_send, l_recv, p_send, p_recv, a_send, a_recv, own_sem, c_send, c_recv, q_send, q_recv, z_send, z_recv,
    zg_send, zg_recv, qg_send, qg_recv, cg_send, cg_recv, o_send, o_recv,
):
    n, nz, members, fields, cells, mloc, grid_cells = dims
    rows = mloc * fields
    nq = n // 2
    total = gram.shape[0]
    half, quart = total // 2, total // 2 // nq
    piece = quart // nz
    norm_factor = math.sqrt(members - 1)
    me, mz = lax.axis_index("mem"), lax.axis_index("cell")
    core, chip = lax.rem(me, 2), lax.div(me, 2)
    mate = me + 1 - 2 * core

    fetch = pltpu.make_async_copy(x, near, near_sem)
    fetch.start()

    barrier = pltpu.get_barrier_semaphore()
    for d in range(1, n):
        pl.semaphore_signal(barrier, inc=1, device_id={"mem": lax.rem(me + d, n)}, device_id_type=MESH)
    for d in range(1, nz):
        pl.semaphore_signal(barrier, inc=1, device_id={"cell": lax.rem(mz + d, nz)}, device_id_type=MESH)
    pl.semaphore_wait(barrier, n - 1 + nz - 1)

    def col(p):
        return pl.ds(pl.multiple_of(p * cells, cells), cells)

    def block(p):
        return pl.ds(pl.multiple_of(p * rows, rows), rows)

    def share(p):
        return pl.ds(pl.multiple_of(p * mloc, mloc), mloc)

    def peer(j):
        return lax.rem(chip + lax.div(j, 2), nq) * 2 + lax.rem(core + j, 2)

    def source(j):
        return lax.rem(chip + nq - lax.div(j, 2), nq) * 2 + lax.rem(core + j, 2)

    def place_copy(p, at):
        return remote(loc, places.at[at], l_send.at[p], l_recv.at[at], {"mem": p})

    def send_places(j, _):
        place_copy(peer(j), me).start()
        return 0

    lax.fori_loop(1, n, send_places, 0)
    places[me] = loc[...]
    obs_rows = loc.shape[0]
    obs = obs_rows * LANES
    fetch.wait()

    def choose(p):
        v = places[p]
        field = jnp.zeros_like(v)
        for f in range(1, fields):
            field = field + jnp.where(v >= f * grid_cells, 1, 0)
        slots = v - field * grid_cells - (mz * n + p) * cells

        def build(i, _):
            at = pl.ds(pl.multiple_of(i * LANES, LANES), LANES)
            cell = iota((LANES, LANES), 0) + i * LANES
            for r in range(obs_rows):
                hot[at, r * LANES:(r + 1) * LANES] = jnp.where(cell == slots[r:r + 1, :], 1.0, 0.0).astype(BF)
            return 0

        lax.fori_loop(0, cells // LANES, build, 0)
        both = nn(near[:, col(p)], hot[...])
        wanted = jnp.concatenate([field[r:r + 1, :] for r in range(obs_rows)], axis=1)
        both = jnp.where((iota((rows, obs), 0) & (fields - 1)) == wanted, both, 0.0).astype(BF)
        low = iota((mloc, rows), 0) * fields
        join = jnp.where((iota((mloc, rows), 1) >= low) & (iota((mloc, rows), 1) < low + fields), 1.0, 0.0)
        return nn(join.astype(BF), both).astype(BF)

    def pick_copy(p, at):
        return remote(picked.at[p], raw.at[share(at)], p_send.at[p], p_recv.at[at], {"mem": p})

    def send_picked(j, _):
        p = peer(j)
        place_copy(p, p).wait_recv()
        picked[p] = choose(p)
        pick_copy(p, me).start()
        return 0

    lax.fori_loop(1, n, send_picked, 0)
    raw[share(me), :] = choose(me)

    def get_picked(j, _):
        p = source(j)
        pick_copy(p, p).wait_recv()
        return 0

    lax.fori_loop(1, n, get_picked, 0)

    errors = jnp.concatenate([spread[r:r + 1, :] for r in range(obs_rows)], axis=1)
    values = jnp.concatenate([datum[r:r + 1, :] for r in range(obs_rows)], axis=1)
    inverse = 1.0 / (errors * norm_factor)

    def add_rows(i, carry):
        at = pl.ds(pl.multiple_of(i * 64, 64), 64)
        return carry + jnp.sum(raw[at, :].astype(F32), axis=0, keepdims=True)

    mean_obs = lax.fori_loop(0, members // 64, add_rows, jnp.zeros((1, obs), F32)) / members
    innovation = ((values - mean_obs) / errors).astype(BF)

    def scale_rows(i, _):
        at = pl.ds(pl.multiple_of(i * 64, 64), 64)
        anomaly = (raw[at, :].astype(F32) - mean_obs).astype(BF)
        scaled[at, :] = (anomaly.astype(F32) * inverse).astype(BF)
        return 0

    lax.fori_loop(0, members // 64, scale_rows, 0)
    spread16 = jnp.where(iota((16, obs), 0) == 0, innovation.astype(F32), 0.0).astype(BF)
    projected = jnp.sum(nt(spread16, scaled[...]), axis=0, keepdims=True)

    nb = members // LANES
    lane, line = iota((LANES, LANES), 1), iota((LANES, LANES), 0)
    place = 0
    for bi in range(nb):
        strip = nt(scaled[bi * LANES:(bi + 1) * LANES, :], scaled[bi * LANES:, :])
        for bj in range(bi, nb):
            blk = strip[:, (bj - bi) * LANES:(bj - bi + 1) * LANES]
            if bi == bj:
                chunk = projected[:, bi * LANES:(bi + 1) * LANES]
                turned = pltpu.roll(jnp.broadcast_to(chunk, (8, LANES)), LANES // 2, 1)[0:1, :]
                low = lane < LANES // 2
                blk = jnp.where(low & (line == LANES - 1), chunk, blk)
                blk = jnp.where(low & (line == LANES - 2), turned, blk)
            gram[place * LANES:(place + 1) * LANES, :] = blk
            place += 1
    if place * LANES < total:
        gram[place * LANES:, :] = jnp.zeros((total - place * LANES, LANES), F32)

    def cut(start, size):
        return pl.ds(pl.multiple_of(start, 8), size)

    go = remote(gram.at[cut((1 - core) * half, half)], r1, c_send, c_recv, {"mem": mate})
    go.start()
    go.wait_recv()
    s1[...] = gram[cut(core * half, half), :] + r1[...]

    def to_chip(d):
        return lax.rem(lax.rem(chip + d, nq) * 2 + core, n)

    def plane(d):
        q = lax.rem(chip + d, nq)
        return remote(s1.at[cut(q * quart, quart)], r2.at[d], q_send.at[d], q_recv.at[d], {"mem": to_chip(d)})

    for d in range(1, nq):
        plane(d).start()
    acc = s1[cut(chip * quart, quart), :]
    for d in range(1, nq):
        plane(d).wait_recv()
        acc = acc + r2[d]
    s2[...] = acc

    def block_copy(p, at):
        return remote(x.at[:, col(p)], held.at[block(at)], a_send.at[p], a_recv.at[at], {"mem": p})

    def take(p):
        got = held[block(p), :]
        for f in range(fields):
            pick = jnp.where(iota((mloc, rows), 1) == iota((mloc, rows), 0) * fields + f, 1.0, 0.0).astype(BF)
            lines = nn(pick, got)
            at = slice(f * cells, (f + 1) * cells)
            anom[share(p), at] = lines.astype(BF)
            means[:, at] += jnp.sum(lines, axis=0, keepdims=True)

    def send_block(j, _):
        block_copy(peer(j), me).start()
        return 0

    def get_block(j, _):
        p = source(j)
        block_copy(p, p).wait_recv()
        take(p)
        return 0

    def line_of(d):
        k = lax.rem(mz + d, nz)
        return remote(s2.at[cut(k * piece, piece)], r3.at[d], z_send.at[d], z_recv.at[d], {"cell": k})

    for d in range(1, nz):
        line_of(d).start()
    lax.fori_loop(1, n, send_block, 0)
    own = pltpu.make_async_copy(x.at[:, col(me)], held.at[block(me)], own_sem)
    own.start()
    means[...] = jnp.zeros_like(means)
    own.wait()
    take(me)
    acc = s2[cut(mz * piece, piece), :]
    for d in range(1, nz):
        line_of(d).wait_recv()
        acc = acc + r3[d]
    mine = core * half + chip * quart
    full[cut(mine + mz * piece, piece), :] = acc

    def line_back(d, k):
        at = full.at[cut(mine + k * piece, piece)]
        return remote(at, at, zg_send.at[d], zg_recv.at[d], {"cell": lax.rem(mz + d, nz)})

    for d in range(1, nz):
        line_back(d, mz).start()
    get_block(1, 0)
    for d in range(1, nz):
        line_back(d, lax.rem(mz + nz - d, nz)).wait_recv()

    def plane_back(d, q):
        at = full.at[cut(core * half + q * quart, quart)]
        return remote(at, at, qg_send.at[d], qg_recv.at[d], {"mem": to_chip(d)})

    def pair_back(d, c, q):
        at = full.at[cut(c * half + q * quart, quart)]
        return remote(at, at, cg_send.at[d], cg_recv.at[d], {"mem": mate})

    for d in range(1, nq):
        plane_back(d, chip).start()
    pair_back(0, core, chip).start()
    for d in range(1, nq):
        q = lax.rem(chip + nq - d, nq)
        plane_back(d, q).wait_recv()
        pair_back(d, core, q).start()
    for d in range(nq):
        pair_back(d, 1 - core, lax.rem(chip + nq - d, nq)).wait_recv()

    place = 0
    squares = jnp.zeros((1, LANES), F32)
    proj = []
    for bi in range(nb):
        for bj in range(bi, nb):
            blk = full[place * LANES:(place + 1) * LANES, :]
            place += 1
            here, there = slice(bi * LANES, (bi + 1) * LANES), slice(bj * LANES, (bj + 1) * LANES)
            if bi == bj:
                first, second = blk[LANES - 1:, :], blk[LANES - 2:LANES - 1, :]
                second = pltpu.roll(jnp.broadcast_to(second, (8, LANES)), LANES // 2, 1)[0:1, :]
                proj.append(jnp.where(iota((1, LANES), 1) < LANES // 2, first, second))
                blk = jnp.where(lane >= line, blk, blk.T) + jnp.where(lane == line, 1.0, 0.0)
                sys_f[here, here] = blk
                squares = squares + jnp.sum(blk * blk, axis=0, keepdims=True)
            else:
                sys_f[here, there] = blk
                sys_f[there, here] = blk.T
                squares = squares + 2.0 * jnp.sum(blk * blk, axis=0, keepdims=True)
    projected = jnp.concatenate(proj, axis=1)
    norm_scale = jnp.sqrt(jnp.sum(squares, axis=1, keepdims=True))
    inv_norm = 1.0 / norm_scale

    IP, IU, IQ, IT, IZ = range(5)
    step = 256 if members % 256 == 0 else LANES
    chunks = members // step

    def keep(slot, at, val):
        hi = val.astype(BF)
        his[slot, at, :] = hi
        los[slot, at, :] = (val - hi.astype(F32)).astype(BF)

    def times(a, b, finish):
        def go(i, _):
            at = pl.ds(pl.multiple_of(i * step, step), step)
            ah, al = his[a, at, :], los[a, at, :]
            finish(at, i, nn(ah, his[b]) + nn(ah, los[b]) + nn(al, his[b]))
            return 0

        lax.fori_loop(0, chunks, go, 0)

    def scale(i, _):
        at = pl.ds(pl.multiple_of(i * 64, 64), 64)
        val = sys_f[at, :] * inv_norm
        sys_f[at, :] = val
        keep(IP, at, val)
        return 0

    lax.fori_loop(0, members // 64, scale, 0)

    def quartic(into):
        def first(at, i, val):
            val = val - 4.5 * sys_f[at, :]
            u_f[at, :] = val
            keep(IU, at, val)

        times(IP, IP, first)

        def second(at, i, val):
            val = 0.0625 * val + 0.421875 * u_f[at, :] - 0.5390625 * sys_f[at, :]
            diagonal = iota((step, members), 1) == iota((step, members), 0) + i * step
            val = val + jnp.where(diagonal, 2.25, 0.0)
            for slot in into:
                keep(slot, at, val)

        times(IU, IU, second)

    def renew():
        times(IQ, IP, lambda at, i, val: keep(IT, at, val))

        def last(at, i, val):
            sys_f[at, :] = val
            keep(IP, at, val)

        times(IQ, IT, last)

    quartic((IQ, IZ))
    renew()

    def pair_turn(turn, _):
        now = IZ + turn
        quartic((IQ,))
        times(IQ, now, lambda at, i, val: keep(now + 1, at, val))
        renew()
        return 0

    lax.fori_loop(0, NS_ITERS // 2 - 2, pair_turn, 0)
    quartic((IQ,))

    def final(at, i, val):
        z_f[at, :] = val

    times(IQ, IZ + NS_ITERS // 2 - 2, final)

    lax.fori_loop(2, n, get_block, 0)
    means[...] = means[...] / members

    def centre(i, _):
        at = pl.ds(pl.multiple_of(i * 64, 64), 64)
        anom[at, :] = (anom[at, :].astype(F32) - means[...]).astype(BF)
        return 0

    lax.fori_loop(0, members // 64, centre, 0)

    root = 1.0 / jnp.sqrt(norm_scale)

    def weigh(i, carry):
        at = pl.ds(pl.multiple_of(i * 64, 64), 64)
        val = z_f[at, :]
        w = (val * root).astype(BF)
        wts[at, :] = w
        shift = jnp.sum(val * projected, axis=1, keepdims=True) * (root * (1.0 / norm_factor))
        return carry + jnp.sum(shift * w.astype(F32), axis=0, keepdims=True)

    mixed = lax.fori_loop(0, members // 64, weigh, jnp.zeros((1, members), F32))
    base[...] = means[...] + row_times(mixed, anom[...])

    def make(p):
        double = jnp.where(
            (iota((rows, mloc), 0) >= iota((rows, mloc), 1) * fields)
            & (iota((rows, mloc), 0) < iota((rows, mloc), 1) * fields + fields), 1.0, 0.0).astype(BF)
        w2 = nn(double, wts[share(p), :]).astype(BF)
        field = iota((rows, cells), 0) & (fields - 1)
        out = None
        for f in range(fields):
            at = slice(f * cells, (f + 1) * cells)
            part = nn(w2, anom[:, at]) + base[:, at]
            out = part if out is None else jnp.where(field == f, part, out)
        return out.astype(BF)

    def out_copy(p, at):
        return remote(outs.at[p], y.at[:, col(at)], o_send.at[p], o_recv.at[at], {"mem": p})

    def send_out(j, _):
        p = peer(j)
        outs[p] = make(p)
        out_copy(p, me).start()
        return 0

    lax.fori_loop(1, n, send_out, 0)
    outs[me] = make(me)
    own = pltpu.make_async_copy(outs.at[me], y.at[:, col(me)], own_sem)
    own.start()

    def finish_out(j, _):
        p = source(j)
        out_copy(p, p).wait_recv()
        return 0

    lax.fori_loop(1, n, finish_out, 0)
    own.wait()

    def sent(j, _):
        p = peer(j)
        place_copy(p, me).wait_send()
        pick_copy(p, me).wait_send()
        block_copy(p, me).wait_send()
        out_copy(p, me).wait_send()
        return 0

    lax.fori_loop(1, n, sent, 0)
    go.wait_send()
    for d in range(1, nq):
        plane(d).wait_send()
        plane_back(d, chip).wait_send()
    for d in range(1, nz):
        line_of(d).wait_send()
        line_back(d, mz).wait_send()
    for d in range(nq):
        pair_back(d, core, lax.rem(chip + nq - d, nq)).wait_send()


def local(prior_ensemble, measurement_location, measurement_datum, measurement_spread):
    n, nz = lax.axis_size("mem"), lax.axis_size("cell")
    mloc, fields, width = prior_ensemble.shape
    members, cells, rows = mloc * n, width // n, mloc * fields
    obs = measurement_location.size
    nb = members // LANES
    unit = 8 * n * nz
    total = -(-(nb * (nb + 1) // 2 * LANES) // unit) * unit
    half, nq = total // 2, n // 2
    quart = half // nq
    piece = quart // nz
    dims = (n, nz, members, fields, cells, mloc, width * nz)
    zslots = 4 + NS_ITERS // 2 - 1
    vm, dma = pltpu.VMEM, pltpu.SemaphoreType.DMA
    square = (members, members)
    scratch = [
        vm((rows, width), BF), vm((n,) + measurement_location.shape, jnp.int32),
        vm((n, mloc, obs), BF), vm((members, obs), BF),
        vm((n * rows, cells), BF), vm((members, fields * cells), BF), vm((1, fields * cells), F32),
        vm((cells, obs), BF), vm((members, obs), BF),
        vm((total, LANES), F32), vm((half, LANES), F32), vm((half, LANES), F32),
        vm((nq, quart, LANES), F32), vm((quart, LANES), F32), vm((nz, piece, LANES), F32),
        vm((total, LANES), F32),
        vm(square, F32), vm(square, F32), vm(square, F32),
        vm((zslots,) + square, BF), vm((zslots,) + square, BF), vm(square, BF),
        vm((1, fields * cells), F32), vm((n, rows, cells), BF),
        dma, dma((n,)), dma((n,)), dma((n,)), dma((n,)),
        dma((n,)), dma((n,)), dma, dma, dma, dma((nq,)), dma((nq,)), dma((nz,)), dma((nz,)),
        dma((nz,)), dma((nz,)), dma((nq,)), dma((nq,)), dma((nq,)), dma((nq,)), dma((n,)), dma((n,)),
    ]
    out = pl.pallas_call(
        functools.partial(kernel, dims),
        out_shape=jax.ShapeDtypeStruct((rows, width), BF),
        in_specs=[pl.BlockSpec(memory_space=pl.ANY)] + [pl.BlockSpec(memory_space=pltpu.VMEM)] * 3,
        out_specs=pl.BlockSpec(memory_space=pl.ANY),
        scratch_shapes=scratch,
        compiler_params=pltpu.CompilerParams(
            collective_id=0, has_side_effects=True, vmem_limit_bytes=50 * 1024 * 1024
        ),
    )(prior_ensemble.reshape(rows, width), measurement_location, measurement_datum, measurement_spread)
    return out.reshape(mloc, fields, width)


def solution(mesh):
    placed = (P("mem", None, "cell"), P("cell", "mem"), P("cell", "mem"), P("cell", "mem"))
    return jax.shard_map(
        local, mesh=mesh, in_specs=placed, out_specs=P("mem", None, "cell"), check_vma=False
    )
```

```python
import functools
import math

import jax
import jax.numpy as jnp
from jax import lax
from jax.experimental import pallas as pl
from jax.experimental.pallas import tpu as pltpu
from jax.sharding import PartitionSpec as P

NS_ITERS = 8
LANES = 128
BF, F32 = jnp.bfloat16, jnp.float32
MESH = pl.DeviceIdType.MESH


def iota(shape, dim):
    return lax.broadcasted_iota(jnp.int32, shape, dim)


def remote(src, dst, send, recv, where):
    return pltpu.make_async_remote_copy(
        src_ref=src, dst_ref=dst, send_sem=send, recv_sem=recv, device_id=where, device_id_type=MESH
    )


def nt(a, b):
    return lax.dot_general(a, b, (((1,), (1,)), ((), ())), preferred_element_type=F32)


def nn(a, b):
    return jnp.dot(a, b, preferred_element_type=F32)


def thirds(v):
    hi = v.astype(BF)
    rest = v - hi.astype(F32)
    mid = rest.astype(BF)
    lo = (rest - mid.astype(F32)).astype(BF)
    return hi, mid, lo


def row_times(v, mat):
    parts = thirds(v)
    row = iota((16, v.shape[1]), 0)
    stack = jnp.zeros((16, v.shape[1]), F32)
    for i, part in enumerate(parts):
        stack = jnp.where(row == i, part.astype(F32), stack)
    return jnp.sum(nn(stack.astype(BF), mat), axis=0, keepdims=True)


def kernel(
    dims, x, loc, datum, spread, y,
    near, places, picked, raw, held, anom, means, hot, scaled, gram, r1, s1, r2, s2, r3, full,
    sys_f, u_f, z_f, his, los, wts, base, outs,
    near_sem, l_send, l_recv, p_send, p_recv, a_send, a_recv, own_sem, c_send, c_recv, q_send, q_recv, z_send, z_recv,
    zg_send, zg_recv, qg_send, qg_recv, cg_send, cg_recv, o_send, o_recv,
):
    n, nz, members, fields, cells, mloc, grid_cells = dims
    rows = mloc * fields
    nq = n // 2
    total = gram.shape[0]
    half, quart = total // 2, total // 2 // nq
    piece = quart // nz
    norm_factor = math.sqrt(members - 1)
    me, mz = lax.axis_index("mem"), lax.axis_index("cell")
    core, chip = lax.rem(me, 2), lax.div(me, 2)
    mate = me + 1 - 2 * core

    fetch = pltpu.make_async_copy(x, near, near_sem)
    fetch.start()

    barrier = pltpu.get_barrier_semaphore()
    for d in range(1, n):
        pl.semaphore_signal(barrier, inc=1, device_id={"mem": lax.rem(me + d, n)}, device_id_type=MESH)
    for d in range(1, nz):
        pl.semaphore_signal(barrier, inc=1, device_id={"cell": lax.rem(mz + d, nz)}, device_id_type=MESH)
    pl.semaphore_wait(barrier, n - 1 + nz - 1)

    def col(p):
        return pl.ds(pl.multiple_of(p * cells, cells), cells)

    def block(p):
        return pl.ds(pl.multiple_of(p * rows, rows), rows)

    def share(p):
        return pl.ds(pl.multiple_of(p * mloc, mloc), mloc)

    def peer(j):
        return lax.rem(chip + lax.div(j, 2), nq) * 2 + lax.rem(core + j, 2)

    def source(j):
        return lax.rem(chip + nq - lax.div(j, 2), nq) * 2 + lax.rem(core + j, 2)

    def place_copy(p, at):
        return remote(loc, places.at[at], l_send.at[p], l_recv.at[at], {"mem": p})

    def send_places(j, _):
        place_copy(peer(j), me).start()
        return 0

    lax.fori_loop(1, n, send_places, 0)
    places[me] = loc[...]
    obs_rows = loc.shape[0]
    obs = obs_rows * LANES
    fetch.wait()

    def choose(p):
        v = places[p]
        field = jnp.zeros_like(v)
        for f in range(1, fields):
            field = field + jnp.where(v >= f * grid_cells, 1, 0)
        slots = v - field * grid_cells - (mz * n + p) * cells

        def build(i, _):
            at = pl.ds(pl.multiple_of(i * LANES, LANES), LANES)
            cell = iota((LANES, LANES), 0) + i * LANES
            for r in range(obs_rows):
                hot[at, r * LANES:(r + 1) * LANES] = jnp.where(cell == slots[r:r + 1, :], 1.0, 0.0).astype(BF)
            return 0

        lax.fori_loop(0, cells // LANES, build, 0)
        both = nn(near[:, col(p)], hot[...])
        wanted = jnp.concatenate([field[r:r + 1, :] for r in range(obs_rows)], axis=1)
        both = jnp.where((iota((rows, obs), 0) & (fields - 1)) == wanted, both, 0.0).astype(BF)
        low = iota((mloc, rows), 0) * fields
        join = jnp.where((iota((mloc, rows), 1) >= low) & (iota((mloc, rows), 1) < low + fields), 1.0, 0.0)
        return nn(join.astype(BF), both).astype(BF)

    def pick_copy(p, at):
        return remote(picked.at[p], raw.at[share(at)], p_send.at[p], p_recv.at[at], {"mem": p})

    def send_picked(j, _):
        p = peer(j)
        place_copy(p, p).wait_recv()
        picked[p] = choose(p)
        pick_copy(p, me).start()
        return 0

    lax.fori_loop(1, n, send_picked, 0)
    raw[share(me), :] = choose(me)

    def get_picked(j, _):
        p = source(j)
        pick_copy(p, p).wait_recv()
        return 0

    lax.fori_loop(1, n, get_picked, 0)

    errors = jnp.concatenate([spread[r:r + 1, :] for r in range(obs_rows)], axis=1)
    values = jnp.concatenate([datum[r:r + 1, :] for r in range(obs_rows)], axis=1)
    inverse = 1.0 / (errors * norm_factor)

    def add_rows(i, carry):
        at = pl.ds(pl.multiple_of(i * 64, 64), 64)
        return carry + jnp.sum(raw[at, :].astype(F32), axis=0, keepdims=True)

    mean_obs = lax.fori_loop(0, members // 64, add_rows, jnp.zeros((1, obs), F32)) / members
    innovation = ((values - mean_obs) / errors).astype(BF)

    def scale_rows(i, _):
        at = pl.ds(pl.multiple_of(i * 64, 64), 64)
        anomaly = (raw[at, :].astype(F32) - mean_obs).astype(BF)
        scaled[at, :] = (anomaly.astype(F32) * inverse).astype(BF)
        return 0

    lax.fori_loop(0, members // 64, scale_rows, 0)
    spread16 = jnp.where(iota((16, obs), 0) == 0, innovation.astype(F32), 0.0).astype(BF)
    projected = jnp.sum(nt(spread16, scaled[...]), axis=0, keepdims=True)

    nb = members // LANES
    lane, line = iota((LANES, LANES), 1), iota((LANES, LANES), 0)
    place = 0
    for bi in range(nb):
        strip = nt(scaled[bi * LANES:(bi + 1) * LANES, :], scaled[bi * LANES:, :])
        for bj in range(bi, nb):
            blk = strip[:, (bj - bi) * LANES:(bj - bi + 1) * LANES]
            if bi == bj:
                chunk = projected[:, bi * LANES:(bi + 1) * LANES]
                turned = pltpu.roll(jnp.broadcast_to(chunk, (8, LANES)), LANES // 2, 1)[0:1, :]
                low = lane < LANES // 2
                blk = jnp.where(low & (line == LANES - 1), chunk, blk)
                blk = jnp.where(low & (line == LANES - 2), turned, blk)
            gram[place * LANES:(place + 1) * LANES, :] = blk
            place += 1
    if place * LANES < total:
        gram[place * LANES:, :] = jnp.zeros((total - place * LANES, LANES), F32)

    def cut(start, size):
        return pl.ds(pl.multiple_of(start, 8), size)

    go = remote(gram.at[cut((1 - core) * half, half)], r1, c_send, c_recv, {"mem": mate})
    go.start()
    go.wait_recv()
    s1[...] = gram[cut(core * half, half), :] + r1[...]

    def to_chip(d):
        return lax.rem(lax.rem(chip + d, nq) * 2 + core, n)

    def plane(d):
        q = lax.rem(chip + d, nq)
        return remote(s1.at[cut(q * quart, quart)], r2.at[d], q_send.at[d], q_recv.at[d], {"mem": to_chip(d)})

    for d in range(1, nq):
        plane(d).start()
    acc = s1[cut(chip * quart, quart), :]
    for d in range(1, nq):
        plane(d).wait_recv()
        acc = acc + r2[d]
    s2[...] = acc

    def block_copy(p, at):
        return remote(x.at[:, col(p)], held.at[block(at)], a_send.at[p], a_recv.at[at], {"mem": p})

    def take(p):
        got = held[block(p), :]
        for f in range(fields):
            pick = jnp.where(iota((mloc, rows), 1) == iota((mloc, rows), 0) * fields + f, 1.0, 0.0).astype(BF)
            lines = nn(pick, got)
            at = slice(f * cells, (f + 1) * cells)
            anom[share(p), at] = lines.astype(BF)
            means[:, at] += jnp.sum(lines, axis=0, keepdims=True)

    def send_block(j, _):
        block_copy(peer(j), me).start()
        return 0

    def get_block(j, _):
        p = source(j)
        block_copy(p, p).wait_recv()
        take(p)
        return 0

    def line_of(d):
        k = lax.rem(mz + d, nz)
        return remote(s2.at[cut(k * piece, piece)], r3.at[d], z_send.at[d], z_recv.at[d], {"cell": k})

    for d in range(1, nz):
        line_of(d).start()
    send_block(1, 0)
    own = pltpu.make_async_copy(x.at[:, col(me)], held.at[block(me)], own_sem)
    own.start()
    means[...] = jnp.zeros_like(means)
    own.wait()
    take(me)
    acc = s2[cut(mz * piece, piece), :]
    for d in range(1, nz):
        line_of(d).wait_recv()
        acc = acc + r3[d]
    mine = core * half + chip * quart
    full[cut(mine + mz * piece, piece), :] = acc

    def line_back(d, k):
        at = full.at[cut(mine + k * piece, piece)]
        return remote(at, at, zg_send.at[d], zg_recv.at[d], {"cell": lax.rem(mz + d, nz)})

    for d in range(1, nz):
        line_back(d, mz).start()
    get_block(1, 0)
    for d in range(1, nz):
        line_back(d, lax.rem(mz + nz - d, nz)).wait_recv()

    def plane_back(d, q):
        at = full.at[cut(core * half + q * quart, quart)]
        return remote(at, at, qg_send.at[d], qg_recv.at[d], {"mem": to_chip(d)})

    def pair_back(d, c, q):
        at = full.at[cut(c * half + q * quart, quart)]
        return remote(at, at, cg_send.at[d], cg_recv.at[d], {"mem": mate})

    for d in range(1, nq):
        plane_back(d, chip).start()
    pair_back(0, core, chip).start()
    for d in range(1, nq):
        q = lax.rem(chip + nq - d, nq)
        plane_back(d, q).wait_recv()
        pair_back(d, core, q).start()
    lax.fori_loop(2, n, send_block, 0)
    for d in range(nq):
        pair_back(d, 1 - core, lax.rem(chip + nq - d, nq)).wait_recv()

    place = 0
    squares = jnp.zeros((1, LANES), F32)
    proj = []
    for bi in range(nb):
        for bj in range(bi, nb):
            blk = full[place * LANES:(place + 1) * LANES, :]
            place += 1
            here, there = slice(bi * LANES, (bi + 1) * LANES), slice(bj * LANES, (bj + 1) * LANES)
            if bi == bj:
                first, second = blk[LANES - 1:, :], blk[LANES - 2:LANES - 1, :]
                second = pltpu.roll(jnp.broadcast_to(second, (8, LANES)), LANES // 2, 1)[0:1, :]
                proj.append(jnp.where(iota((1, LANES), 1) < LANES // 2, first, second))
                blk = jnp.where(lane >= line, blk, blk.T) + jnp.where(lane == line, 1.0, 0.0)
                sys_f[here, here] = blk
                squares = squares + jnp.sum(blk * blk, axis=0, keepdims=True)
            else:
                sys_f[here, there] = blk
                sys_f[there, here] = blk.T
                squares = squares + 2.0 * jnp.sum(blk * blk, axis=0, keepdims=True)
    projected = jnp.concatenate(proj, axis=1)
    norm_scale = jnp.sqrt(jnp.sum(squares, axis=1, keepdims=True))
    inv_norm = 1.0 / norm_scale

    IP, IU, IQ, IT, IZ = range(5)
    step = 256 if members % 256 == 0 else LANES
    chunks = members // step

    def keep(slot, at, val):
        hi = val.astype(BF)
        his[slot, at, :] = hi
        los[slot, at, :] = (val - hi.astype(F32)).astype(BF)

    def times(a, b, finish):
        def go(i, _):
            at = pl.ds(pl.multiple_of(i * step, step), step)
            ah, al = his[a, at, :], los[a, at, :]
            finish(at, i, nn(ah, his[b]) + nn(ah, los[b]) + nn(al, his[b]))
            return 0

        lax.fori_loop(0, chunks, go, 0)

    def scale(i, _):
        at = pl.ds(pl.multiple_of(i * 64, 64), 64)
        val = sys_f[at, :] * inv_norm
        sys_f[at, :] = val
        keep(IP, at, val)
        return 0

    lax.fori_loop(0, members // 64, scale, 0)

    def quartic(into):
        def first(at, i, val):
            val = val - 4.5 * sys_f[at, :]
            u_f[at, :] = val
            keep(IU, at, val)

        times(IP, IP, first)

        def second(at, i, val):
            val = 0.0625 * val + 0.421875 * u_f[at, :] - 0.5390625 * sys_f[at, :]
            diagonal = iota((step, members), 1) == iota((step, members), 0) + i * step
            val = val + jnp.where(diagonal, 2.25, 0.0)
            for slot in into:
                keep(slot, at, val)

        times(IU, IU, second)

    def renew():
        times(IQ, IP, lambda at, i, val: keep(IT, at, val))

        def last(at, i, val):
            sys_f[at, :] = val
            keep(IP, at, val)

        times(IQ, IT, last)

    quartic((IQ, IZ))
    renew()

    def pair_turn(turn, _):
        now = IZ + turn
        quartic((IQ,))
        times(IQ, now, lambda at, i, val: keep(now + 1, at, val))
        renew()
        return 0

    lax.fori_loop(0, NS_ITERS // 2 - 2, pair_turn, 0)
    quartic((IQ,))

    def final(at, i, val):
        z_f[at, :] = val

    times(IQ, IZ + NS_ITERS // 2 - 2, final)

    lax.fori_loop(2, n, get_block, 0)
    means[...] = means[...] / members

    def centre(i, _):
        at = pl.ds(pl.multiple_of(i * 64, 64), 64)
        anom[at, :] = (anom[at, :].astype(F32) - means[...]).astype(BF)
        return 0

    lax.fori_loop(0, members // 64, centre, 0)

    root = 1.0 / jnp.sqrt(norm_scale)

    def weigh(i, carry):
        at = pl.ds(pl.multiple_of(i * 64, 64), 64)
        val = z_f[at, :]
        w = (val * root).astype(BF)
        wts[at, :] = w
        shift = jnp.sum(val * projected, axis=1, keepdims=True) * (root * (1.0 / norm_factor))
        return carry + jnp.sum(shift * w.astype(F32), axis=0, keepdims=True)

    mixed = lax.fori_loop(0, members // 64, weigh, jnp.zeros((1, members), F32))
    base[...] = means[...] + row_times(mixed, anom[...])

    def make(p):
        double = jnp.where(
            (iota((rows, mloc), 0) >= iota((rows, mloc), 1) * fields)
            & (iota((rows, mloc), 0) < iota((rows, mloc), 1) * fields + fields), 1.0, 0.0).astype(BF)
        w2 = nn(double, wts[share(p), :]).astype(BF)
        field = iota((rows, cells), 0) & (fields - 1)
        out = None
        for f in range(fields):
            at = slice(f * cells, (f + 1) * cells)
            part = nn(w2, anom[:, at]) + base[:, at]
            out = part if out is None else jnp.where(field == f, part, out)
        return out.astype(BF)

    def out_copy(p, at):
        return remote(outs.at[p], y.at[:, col(at)], o_send.at[p], o_recv.at[at], {"mem": p})

    def send_out(j, _):
        p = peer(j)
        outs[p] = make(p)
        out_copy(p, me).start()
        return 0

    lax.fori_loop(1, n, send_out, 0)
    outs[me] = make(me)
    own = pltpu.make_async_copy(outs.at[me], y.at[:, col(me)], own_sem)
    own.start()

    def finish_out(j, _):
        p = source(j)
        out_copy(p, p).wait_recv()
        return 0

    lax.fori_loop(1, n, finish_out, 0)
    own.wait()

    def sent(j, _):
        p = peer(j)
        place_copy(p, me).wait_send()
        pick_copy(p, me).wait_send()
        block_copy(p, me).wait_send()
        out_copy(p, me).wait_send()
        return 0

    lax.fori_loop(1, n, sent, 0)
    go.wait_send()
    for d in range(1, nq):
        plane(d).wait_send()
        plane_back(d, chip).wait_send()
    for d in range(1, nz):
        line_of(d).wait_send()
        line_back(d, mz).wait_send()
    for d in range(nq):
        pair_back(d, core, lax.rem(chip + nq - d, nq)).wait_send()


def local(prior_ensemble, measurement_location, measurement_datum, measurement_spread):
    n, nz = lax.axis_size("mem"), lax.axis_size("cell")
    mloc, fields, width = prior_ensemble.shape
    members, cells, rows = mloc * n, width // n, mloc * fields
    obs = measurement_location.size
    nb = members // LANES
    unit = 8 * n * nz
    total = -(-(nb * (nb + 1) // 2 * LANES) // unit) * unit
    half, nq = total // 2, n // 2
    quart = half // nq
    piece = quart // nz
    dims = (n, nz, members, fields, cells, mloc, width * nz)
    zslots = 4 + NS_ITERS // 2 - 1
    vm, dma = pltpu.VMEM, pltpu.SemaphoreType.DMA
    square = (members, members)
    scratch = [
        vm((rows, width), BF), vm((n,) + measurement_location.shape, jnp.int32),
        vm((n, mloc, obs), BF), vm((members, obs), BF),
        vm((n * rows, cells), BF), vm((members, fields * cells), BF), vm((1, fields * cells), F32),
        vm((cells, obs), BF), vm((members, obs), BF),
        vm((total, LANES), F32), vm((half, LANES), F32), vm((half, LANES), F32),
        vm((nq, quart, LANES), F32), vm((quart, LANES), F32), vm((nz, piece, LANES), F32),
        vm((total, LANES), F32),
        vm(square, F32), vm(square, F32), vm(square, F32),
        vm((zslots,) + square, BF), vm((zslots,) + square, BF), vm(square, BF),
        vm((1, fields * cells), F32), vm((n, rows, cells), BF),
        dma, dma((n,)), dma((n,)), dma((n,)), dma((n,)),
        dma((n,)), dma((n,)), dma, dma, dma, dma((nq,)), dma((nq,)), dma((nz,)), dma((nz,)),
        dma((nz,)), dma((nz,)), dma((nq,)), dma((nq,)), dma((nq,)), dma((nq,)), dma((n,)), dma((n,)),
    ]
    out = pl.pallas_call(
        functools.partial(kernel, dims),
        out_shape=jax.ShapeDtypeStruct((rows, width), BF),
        in_specs=[pl.BlockSpec(memory_space=pl.ANY)] + [pl.BlockSpec(memory_space=pltpu.VMEM)] * 3,
        out_specs=pl.BlockSpec(memory_space=pl.ANY),
        scratch_shapes=scratch,
        compiler_params=pltpu.CompilerParams(
            collective_id=0, has_side_effects=True, vmem_limit_bytes=50 * 1024 * 1024
        ),
    )(prior_ensemble.reshape(rows, width), measurement_location, measurement_datum, measurement_spread)
    return out.reshape(mloc, fields, width)


def solution(mesh):
    placed = (P("mem", None, "cell"), P("cell", "mem"), P("cell", "mem"), P("cell", "mem"))
    return jax.shard_map(
        local, mesh=mesh, in_specs=placed, out_specs=P("mem", None, "cell"), check_vma=False
    )
```

```python
import functools
import math

import jax
import jax.numpy as jnp
from jax import lax
from jax.experimental import pallas as pl
from jax.experimental.pallas import tpu as pltpu
from jax.sharding import PartitionSpec as P

NS_ITERS = 8
LANES = 128
BF, F32 = jnp.bfloat16, jnp.float32
MESH = pl.DeviceIdType.MESH


def iota(shape, dim):
    return lax.broadcasted_iota(jnp.int32, shape, dim)


def remote(src, dst, send, recv, where):
    return pltpu.make_async_remote_copy(
        src_ref=src, dst_ref=dst, send_sem=send, recv_sem=recv, device_id=where, device_id_type=MESH
    )


def nt(a, b):
    return lax.dot_general(a, b, (((1,), (1,)), ((), ())), preferred_element_type=F32)


def nn(a, b):
    return jnp.dot(a, b, preferred_element_type=F32)


def thirds(v):
    hi = v.astype(BF)
    rest = v - hi.astype(F32)
    mid = rest.astype(BF)
    lo = (rest - mid.astype(F32)).astype(BF)
    return hi, mid, lo


def row_times(v, mat):
    parts = thirds(v)
    row = iota((16, v.shape[1]), 0)
    stack = jnp.zeros((16, v.shape[1]), F32)
    for i, part in enumerate(parts):
        stack = jnp.where(row == i, part.astype(F32), stack)
    return jnp.sum(nn(stack.astype(BF), mat), axis=0, keepdims=True)


def kernel(
    dims, x, loc, datum, spread, y,
    near, places, picked, raw, held, anom, means, hot, scaled, gram, r1, s1, r2, s2, r3, full,
    sys_f, u_f, z_f, his, los, wts, base, outs,
    near_sem, l_send, l_recv, p_send, p_recv, a_send, a_recv, own_sem, c_send, c_recv, q_send, q_recv, z_send, z_recv,
    zg_send, zg_recv, qg_send, qg_recv, cg_send, cg_recv, o_send, o_recv,
):
    n, nz, members, fields, cells, mloc, grid_cells = dims
    rows = mloc * fields
    nq = n // 2
    total = gram.shape[0]
    half, quart = total // 2, total // 2 // nq
    piece = quart // nz
    norm_factor = math.sqrt(members - 1)
    me, mz = lax.axis_index("mem"), lax.axis_index("cell")
    core, chip = lax.rem(me, 2), lax.div(me, 2)
    mate = me + 1 - 2 * core

    fetch = pltpu.make_async_copy(x, near, near_sem)
    fetch.start()

    barrier = pltpu.get_barrier_semaphore()
    for d in range(1, n):
        pl.semaphore_signal(barrier, inc=1, device_id={"mem": lax.rem(me + d, n)}, device_id_type=MESH)
    for d in range(1, nz):
        pl.semaphore_signal(barrier, inc=1, device_id={"cell": lax.rem(mz + d, nz)}, device_id_type=MESH)
    pl.semaphore_wait(barrier, n - 1 + nz - 1)

    def col(p):
        return pl.ds(pl.multiple_of(p * cells, cells), cells)

    def block(p):
        return pl.ds(pl.multiple_of(p * rows, rows), rows)

    def share(p):
        return pl.ds(pl.multiple_of(p * mloc, mloc), mloc)

    def peer(j):
        return lax.rem(chip + lax.div(j, 2), nq) * 2 + lax.rem(core + j, 2)

    def source(j):
        return lax.rem(chip + nq - lax.div(j, 2), nq) * 2 + lax.rem(core + j, 2)

    def place_copy(p, at):
        return remote(loc, places.at[at], l_send.at[p], l_recv.at[at], {"mem": p})

    def send_places(j, _):
        place_copy(peer(j), me).start()
        return 0

    lax.fori_loop(1, n, send_places, 0)
    places[me] = loc[...]
    obs_rows = loc.shape[0]
    obs = obs_rows * LANES
    fetch.wait()

    def choose(p):
        v = places[p]
        field = jnp.zeros_like(v)
        for f in range(1, fields):
            field = field + jnp.where(v >= f * grid_cells, 1, 0)
        slots = v - field * grid_cells - (mz * n + p) * cells

        def build(i, _):
            at = pl.ds(pl.multiple_of(i * LANES, LANES), LANES)
            cell = iota((LANES, LANES), 0) + i * LANES
            for r in range(obs_rows):
                hot[at, r * LANES:(r + 1) * LANES] = jnp.where(cell == slots[r:r + 1, :], 1.0, 0.0).astype(BF)
            return 0

        lax.fori_loop(0, cells // LANES, build, 0)
        both = nn(near[:, col(p)], hot[...])
        wanted = jnp.concatenate([field[r:r + 1, :] for r in range(obs_rows)], axis=1)
        both = jnp.where((iota((rows, obs), 0) & (fields - 1)) == wanted, both, 0.0).astype(BF)
        low = iota((mloc, rows), 0) * fields
        join = jnp.where((iota((mloc, rows), 1) >= low) & (iota((mloc, rows), 1) < low + fields), 1.0, 0.0)
        return nn(join.astype(BF), both).astype(BF)

    def pick_copy(p, at):
        return remote(picked.at[p], raw.at[share(at)], p_send.at[p], p_recv.at[at], {"mem": p})

    def send_picked(j, _):
        p = peer(j)
        place_copy(p, p).wait_recv()
        picked[p] = choose(p)
        pick_copy(p, me).start()
        return 0

    lax.fori_loop(1, n, send_picked, 0)
    raw[share(me), :] = choose(me)

    def get_picked(j, _):
        p = source(j)
        pick_copy(p, p).wait_recv()
        return 0

    lax.fori_loop(1, n, get_picked, 0)

    errors = jnp.concatenate([spread[r:r + 1, :] for r in range(obs_rows)], axis=1)
    values = jnp.concatenate([datum[r:r + 1, :] for r in range(obs_rows)], axis=1)
    inverse = 1.0 / (errors * norm_factor)

    def add_rows(i, carry):
        at = pl.ds(pl.multiple_of(i * 64, 64), 64)
        return carry + jnp.sum(raw[at, :].astype(F32), axis=0, keepdims=True)

    mean_obs = lax.fori_loop(0, members // 64, add_rows, jnp.zeros((1, obs), F32)) / members
    innovation = ((values - mean_obs) / errors).astype(BF)

    def scale_rows(i, _):
        at = pl.ds(pl.multiple_of(i * 64, 64), 64)
        anomaly = (raw[at, :].astype(F32) - mean_obs).astype(BF)
        scaled[at, :] = (anomaly.astype(F32) * inverse).astype(BF)
        return 0

    lax.fori_loop(0, members // 64, scale_rows, 0)
    spread16 = jnp.where(iota((16, obs), 0) == 0, innovation.astype(F32), 0.0).astype(BF)
    projected = jnp.sum(nt(spread16, scaled[...]), axis=0, keepdims=True)

    nb = members // LANES
    lane, line = iota((LANES, LANES), 1), iota((LANES, LANES), 0)
    place = 0
    for bi in range(nb):
        strip = nt(scaled[bi * LANES:(bi + 1) * LANES, :], scaled[bi * LANES:, :])
        for bj in range(bi, nb):
            blk = strip[:, (bj - bi) * LANES:(bj - bi + 1) * LANES]
            if bi == bj:
                chunk = projected[:, bi * LANES:(bi + 1) * LANES]
                turned = pltpu.roll(jnp.broadcast_to(chunk, (8, LANES)), LANES // 2, 1)[0:1, :]
                low = lane < LANES // 2
                blk = jnp.where(low & (line == LANES - 1), chunk, blk)
                blk = jnp.where(low & (line == LANES - 2), turned, blk)
            gram[place * LANES:(place + 1) * LANES, :] = blk
            place += 1
    if place * LANES < total:
        gram[place * LANES:, :] = jnp.zeros((total - place * LANES, LANES), F32)

    def cut(start, size):
        return pl.ds(pl.multiple_of(start, 8), size)

    go = remote(gram.at[cut((1 - core) * half, half)], r1, c_send, c_recv, {"mem": mate})
    go.start()
    go.wait_recv()
    s1[...] = gram[cut(core * half, half), :] + r1[...]

    def to_chip(d):
        return lax.rem(lax.rem(chip + d, nq) * 2 + core, n)

    def plane(d):
        q = lax.rem(chip + d, nq)
        return remote(s1.at[cut(q * quart, quart)], r2.at[d], q_send.at[d], q_recv.at[d], {"mem": to_chip(d)})

    for d in range(1, nq):
        plane(d).start()
    acc = s1[cut(chip * quart, quart), :]
    for d in range(1, nq):
        plane(d).wait_recv()
        acc = acc + r2[d]
    s2[...] = acc

    def block_copy(p, at):
        return remote(x.at[:, col(p)], held.at[block(at)], a_send.at[p], a_recv.at[at], {"mem": p})

    def take(p):
        got = held[block(p), :]
        for f in range(fields):
            pick = jnp.where(iota((mloc, rows), 1) == iota((mloc, rows), 0) * fields + f, 1.0, 0.0).astype(BF)
            lines = nn(pick, got)
            at = slice(f * cells, (f + 1) * cells)
            anom[share(p), at] = lines.astype(BF)
            means[:, at] += jnp.sum(lines, axis=0, keepdims=True)

    def send_block(j, _):
        block_copy(peer(j), me).start()
        return 0

    def get_block(j, _):
        p = source(j)
        block_copy(p, p).wait_recv()
        take(p)
        return 0

    def line_of(d):
        k = lax.rem(mz + d, nz)
        return remote(s2.at[cut(k * piece, piece)], r3.at[d], z_send.at[d], z_recv.at[d], {"cell": k})

    for d in range(1, nz):
        line_of(d).start()
    send_block(1, 0)
    own = pltpu.make_async_copy(x.at[:, col(me)], held.at[block(me)], own_sem)
    own.start()
    means[...] = jnp.zeros_like(means)
    own.wait()
    take(me)
    acc = s2[cut(mz * piece, piece), :]
    for d in range(1, nz):
        line_of(d).wait_recv()
        acc = acc + r3[d]
    mine = core * half + chip * quart
    full[cut(mine + mz * piece, piece), :] = acc

    def line_back(d, k):
        at = full.at[cut(mine + k * piece, piece)]
        return remote(at, at, zg_send.at[d], zg_recv.at[d], {"cell": lax.rem(mz + d, nz)})

    for d in range(1, nz):
        line_back(d, mz).start()
    get_block(1, 0)
    for d in range(1, nz):
        line_back(d, lax.rem(mz + nz - d, nz)).wait_recv()

    def plane_back(d, q):
        at = full.at[cut(core * half + q * quart, quart)]
        return remote(at, at, qg_send.at[d], qg_recv.at[d], {"mem": to_chip(d)})

    def pair_back(d, c, q):
        at = full.at[cut(c * half + q * quart, quart)]
        return remote(at, at, cg_send.at[d], cg_recv.at[d], {"mem": mate})

    for d in range(1, nq):
        plane_back(d, chip).start()
    pair_back(0, core, chip).start()
    for d in range(1, nq):
        q = lax.rem(chip + nq - d, nq)
        plane_back(d, q).wait_recv()
        pair_back(d, core, q).start()
    lax.fori_loop(2, n, send_block, 0)
    for d in range(nq):
        pair_back(d, 1 - core, lax.rem(chip + nq - d, nq)).wait_recv()

    place = 0
    squares = jnp.zeros((1, LANES), F32)
    proj = []
    for bi in range(nb):
        for bj in range(bi, nb):
            blk = full[place * LANES:(place + 1) * LANES, :]
            place += 1
            here, there = slice(bi * LANES, (bi + 1) * LANES), slice(bj * LANES, (bj + 1) * LANES)
            if bi == bj:
                first, second = blk[LANES - 1:, :], blk[LANES - 2:LANES - 1, :]
                second = pltpu.roll(jnp.broadcast_to(second, (8, LANES)), LANES // 2, 1)[0:1, :]
                proj.append(jnp.where(iota((1, LANES), 1) < LANES // 2, first, second))
                blk = jnp.where(lane >= line, blk, blk.T) + jnp.where(lane == line, 1.0, 0.0)
                sys_f[here, here] = blk
                squares = squares + jnp.sum(blk * blk, axis=0, keepdims=True)
            else:
                sys_f[here, there] = blk
                sys_f[there, here] = blk.T
                squares = squares + 2.0 * jnp.sum(blk * blk, axis=0, keepdims=True)
    projected = jnp.concatenate(proj, axis=1)
    norm_scale = jnp.sqrt(jnp.sum(squares, axis=1, keepdims=True))
    inv_norm = 1.0 / norm_scale

    IP, IU, IQ, IT, IZ = range(5)
    step = 256 if members % 256 == 0 else LANES
    chunks = members // step

    def keep(slot, at, val):
        hi = val.astype(BF)
        his[slot, at, :] = hi
        los[slot, at, :] = (val - hi.astype(F32)).astype(BF)

    def times(a, b, finish):
        right = jnp.concatenate([his[b], los[b], his[b]], axis=0)
        for i in range(chunks):
            at = slice(i * step, (i + 1) * step)
            ah, al = his[a, at, :], los[a, at, :]
            finish(at, i, nn(jnp.concatenate([ah, ah, al], axis=1), right))

    def scale(i, _):
        at = pl.ds(pl.multiple_of(i * 64, 64), 64)
        val = sys_f[at, :] * inv_norm
        sys_f[at, :] = val
        keep(IP, at, val)
        return 0

    lax.fori_loop(0, members // 64, scale, 0)

    def quartic(into):
        def first(at, i, val):
            val = val - 4.5 * sys_f[at, :]
            u_f[at, :] = val
            keep(IU, at, val)

        times(IP, IP, first)

        def second(at, i, val):
            val = 0.0625 * val + 0.421875 * u_f[at, :] - 0.5390625 * sys_f[at, :]
            diagonal = iota((step, members), 1) == iota((step, members), 0) + i * step
            val = val + jnp.where(diagonal, 2.25, 0.0)
            for slot in into:
                keep(slot, at, val)

        times(IU, IU, second)

    def renew():
        times(IQ, IP, lambda at, i, val: keep(IT, at, val))

        def last(at, i, val):
            sys_f[at, :] = val
            keep(IP, at, val)

        times(IQ, IT, last)

    quartic((IQ, IZ))
    renew()

    def pair_turn(turn, _):
        now = IZ + turn
        quartic((IQ,))
        times(IQ, now, lambda at, i, val: keep(now + 1, at, val))
        renew()
        return 0

    lax.fori_loop(0, NS_ITERS // 2 - 2, pair_turn, 0)
    quartic((IQ,))

    def final(at, i, val):
        z_f[at, :] = val

    times(IQ, IZ + NS_ITERS // 2 - 2, final)

    lax.fori_loop(2, n, get_block, 0)
    means[...] = means[...] / members

    def centre(i, _):
        at = pl.ds(pl.multiple_of(i * 64, 64), 64)
        anom[at, :] = (anom[at, :].astype(F32) - means[...]).astype(BF)
        return 0

    lax.fori_loop(0, members // 64, centre, 0)

    root = 1.0 / jnp.sqrt(norm_scale)

    def weigh(i, carry):
        at = pl.ds(pl.multiple_of(i * 64, 64), 64)
        val = z_f[at, :]
        w = (val * root).astype(BF)
        wts[at, :] = w
        shift = jnp.sum(val * projected, axis=1, keepdims=True) * (root * (1.0 / norm_factor))
        return carry + jnp.sum(shift * w.astype(F32), axis=0, keepdims=True)

    mixed = lax.fori_loop(0, members // 64, weigh, jnp.zeros((1, members), F32))
    base[...] = means[...] + row_times(mixed, anom[...])

    def make(p):
        double = jnp.where(
            (iota((rows, mloc), 0) >= iota((rows, mloc), 1) * fields)
            & (iota((rows, mloc), 0) < iota((rows, mloc), 1) * fields + fields), 1.0, 0.0).astype(BF)
        w2 = nn(double, wts[share(p), :]).astype(BF)
        field = iota((rows, cells), 0) & (fields - 1)
        out = None
        for f in range(fields):
            at = slice(f * cells, (f + 1) * cells)
            part = nn(w2, anom[:, at]) + base[:, at]
            out = part if out is None else jnp.where(field == f, part, out)
        return out.astype(BF)

    def out_copy(p, at):
        return remote(outs.at[p], y.at[:, col(at)], o_send.at[p], o_recv.at[at], {"mem": p})

    def send_out(j, _):
        p = peer(j)
        outs[p] = make(p)
        out_copy(p, me).start()
        return 0

    lax.fori_loop(1, n, send_out, 0)
    outs[me] = make(me)
    own = pltpu.make_async_copy(outs.at[me], y.at[:, col(me)], own_sem)
    own.start()

    def finish_out(j, _):
        p = source(j)
        out_copy(p, p).wait_recv()
        return 0

    lax.fori_loop(1, n, finish_out, 0)
    own.wait()

    def sent(j, _):
        p = peer(j)
        place_copy(p, me).wait_send()
        pick_copy(p, me).wait_send()
        block_copy(p, me).wait_send()
        out_copy(p, me).wait_send()
        return 0

    lax.fori_loop(1, n, sent, 0)
    go.wait_send()
    for d in range(1, nq):
        plane(d).wait_send()
        plane_back(d, chip).wait_send()
    for d in range(1, nz):
        line_of(d).wait_send()
        line_back(d, mz).wait_send()
    for d in range(nq):
        pair_back(d, core, lax.rem(chip + nq - d, nq)).wait_send()


def local(prior_ensemble, measurement_location, measurement_datum, measurement_spread):
    n, nz = lax.axis_size("mem"), lax.axis_size("cell")
    mloc, fields, width = prior_ensemble.shape
    members, cells, rows = mloc * n, width // n, mloc * fields
    obs = measurement_location.size
    nb = members // LANES
    unit = 8 * n * nz
    total = -(-(nb * (nb + 1) // 2 * LANES) // unit) * unit
    half, nq = total // 2, n // 2
    quart = half // nq
    piece = quart // nz
    dims = (n, nz, members, fields, cells, mloc, width * nz)
    zslots = 4 + NS_ITERS // 2 - 1
    vm, dma = pltpu.VMEM, pltpu.SemaphoreType.DMA
    square = (members, members)
    scratch = [
        vm((rows, width), BF), vm((n,) + measurement_location.shape, jnp.int32),
        vm((n, mloc, obs), BF), vm((members, obs), BF),
        vm((n * rows, cells), BF), vm((members, fields * cells), BF), vm((1, fields * cells), F32),
        vm((cells, obs), BF), vm((members, obs), BF),
        vm((total, LANES), F32), vm((half, LANES), F32), vm((half, LANES), F32),
        vm((nq, quart, LANES), F32), vm((quart, LANES), F32), vm((nz, piece, LANES), F32),
        vm((total, LANES), F32),
        vm(square, F32), vm(square, F32), vm(square, F32),
        vm((zslots,) + square, BF), vm((zslots,) + square, BF), vm(square, BF),
        vm((1, fields * cells), F32), vm((n, rows, cells), BF),
        dma, dma((n,)), dma((n,)), dma((n,)), dma((n,)),
        dma((n,)), dma((n,)), dma, dma, dma, dma((nq,)), dma((nq,)), dma((nz,)), dma((nz,)),
        dma((nz,)), dma((nz,)), dma((nq,)), dma((nq,)), dma((nq,)), dma((nq,)), dma((n,)), dma((n,)),
    ]
    out = pl.pallas_call(
        functools.partial(kernel, dims),
        out_shape=jax.ShapeDtypeStruct((rows, width), BF),
        in_specs=[pl.BlockSpec(memory_space=pl.ANY)] + [pl.BlockSpec(memory_space=pltpu.VMEM)] * 3,
        out_specs=pl.BlockSpec(memory_space=pl.ANY),
        scratch_shapes=scratch,
        compiler_params=pltpu.CompilerParams(
            collective_id=0, has_side_effects=True, vmem_limit_bytes=50 * 1024 * 1024
        ),
    )(prior_ensemble.reshape(rows, width), measurement_location, measurement_datum, measurement_spread)
    return out.reshape(mloc, fields, width)


def solution(mesh):
    placed = (P("mem", None, "cell"), P("cell", "mem"), P("cell", "mem"), P("cell", "mem"))
    return jax.shard_map(
        local, mesh=mesh, in_specs=placed, out_specs=P("mem", None, "cell"), check_vma=False
    )
```

```python
import functools
import math

import jax
import jax.numpy as jnp
from jax import lax
from jax.experimental import pallas as pl
from jax.experimental.pallas import tpu as pltpu
from jax.sharding import PartitionSpec as P

NS_ITERS = 8
LANES = 128
BF, F32 = jnp.bfloat16, jnp.float32
MESH = pl.DeviceIdType.MESH


def iota(shape, dim):
    return lax.broadcasted_iota(jnp.int32, shape, dim)


def remote(src, dst, send, recv, where):
    return pltpu.make_async_remote_copy(
        src_ref=src, dst_ref=dst, send_sem=send, recv_sem=recv, device_id=where, device_id_type=MESH
    )


def nt(a, b):
    return lax.dot_general(a, b, (((1,), (1,)), ((), ())), preferred_element_type=F32)


def nn(a, b):
    return jnp.dot(a, b, preferred_element_type=F32)


def thirds(v):
    hi = v.astype(BF)
    rest = v - hi.astype(F32)
    mid = rest.astype(BF)
    lo = (rest - mid.astype(F32)).astype(BF)
    return hi, mid, lo


def kernel(
    dims, x, loc, datum, spread, y,
    near, places, picked, raw, held, anom, means, scaled, gram, r1, s1, r2, s2, r3, full,
    sys_f, u_f, z_f, his, los, wts, mix, outs,
    near_sem, l_send, l_recv, p_send, p_recv, a_send, a_recv, own_sem, c_send, c_recv, q_send, q_recv, z_send, z_recv,
    zg_send, zg_recv, qg_send, qg_recv, cg_send, cg_recv, o_send, o_recv,
):
    n, nz, members, fields, cells, mloc, grid_cells = dims
    rows = mloc * fields
    nq = n // 2
    total = gram.shape[0]
    half, quart = total // 2, total // 2 // nq
    piece = quart // nz
    norm_factor = math.sqrt(members - 1)
    me, mz = lax.axis_index("mem"), lax.axis_index("cell")
    core, chip = lax.rem(me, 2), lax.div(me, 2)
    mate = me + 1 - 2 * core

    fetch = pltpu.make_async_copy(x, near, near_sem)
    fetch.start()

    barrier = pltpu.get_barrier_semaphore()
    for d in range(1, n):
        pl.semaphore_signal(barrier, inc=1, device_id={"mem": lax.rem(me + d, n)}, device_id_type=MESH)
    for d in range(1, nz):
        pl.semaphore_signal(barrier, inc=1, device_id={"cell": lax.rem(mz + d, nz)}, device_id_type=MESH)
    pl.semaphore_wait(barrier, n - 1 + nz - 1)

    def col(p):
        return pl.ds(pl.multiple_of(p * cells, cells), cells)

    def block(p):
        return pl.ds(pl.multiple_of(p * rows, rows), rows)

    def share(p):
        return pl.ds(pl.multiple_of(p * mloc, mloc), mloc)

    def peer(j):
        return lax.rem(chip + lax.div(j, 2), nq) * 2 + lax.rem(core + j, 2)

    def source(j):
        return lax.rem(chip + nq - lax.div(j, 2), nq) * 2 + lax.rem(core + j, 2)

    def place_copy(p, at):
        return remote(loc, places.at[at], l_send.at[p], l_recv.at[at], {"mem": p})

    def send_places(j, _):
        place_copy(peer(j), me).start()
        return 0

    lax.fori_loop(1, n, send_places, 0)
    places[me] = loc[...]
    obs_rows = loc.shape[0]
    obs = obs_rows * LANES
    fetch.wait()

    def choose(p):
        v = places[p]
        field = jnp.zeros_like(v)
        for f in range(1, fields):
            field = field + jnp.where(v >= f * grid_cells, 1, 0)
        slots = v - field * grid_cells - (mz * n + p) * cells

        slot = jnp.concatenate([slots[r:r + 1, :] for r in range(obs_rows)], axis=1)
        hot = jnp.where(iota((cells, obs), 0) == slot, 1.0, 0.0).astype(BF)
        both = nn(near[:, col(p)], hot)
        wanted = jnp.concatenate([field[r:r + 1, :] for r in range(obs_rows)], axis=1)
        both = jnp.where((iota((rows, obs), 0) & (fields - 1)) == wanted, both, 0.0).astype(BF)
        low = iota((mloc, rows), 0) * fields
        join = jnp.where((iota((mloc, rows), 1) >= low) & (iota((mloc, rows), 1) < low + fields), 1.0, 0.0)
        return nn(join.astype(BF), both).astype(BF)

    def pick_copy(p, at):
        return remote(picked.at[p], raw.at[share(at)], p_send.at[p], p_recv.at[at], {"mem": p})

    def send_picked(i, _):
        p, q = peer(2 * i + 1), peer(2 * i + 2)
        place_copy(p, p).wait_recv()
        place_copy(q, q).wait_recv()
        first, second = choose(p), choose(q)
        picked[p] = first
        picked[q] = second
        pick_copy(p, me).start()
        pick_copy(q, me).start()
        return 0

    lax.fori_loop(0, n // 2 - 1, send_picked, 0)
    p = peer(n - 1)
    place_copy(p, p).wait_recv()
    first, second = choose(p), choose(me)
    picked[p] = first
    pick_copy(p, me).start()
    raw[share(me), :] = second

    def get_picked(j, _):
        p = source(j)
        pick_copy(p, p).wait_recv()
        return 0

    lax.fori_loop(1, n, get_picked, 0)

    errors = jnp.concatenate([spread[r:r + 1, :] for r in range(obs_rows)], axis=1)
    values = jnp.concatenate([datum[r:r + 1, :] for r in range(obs_rows)], axis=1)
    inverse = 1.0 / (errors * norm_factor)

    def add_rows(i, carry):
        at = pl.ds(pl.multiple_of(i * 64, 64), 64)
        return carry + jnp.sum(raw[at, :].astype(F32), axis=0, keepdims=True)

    mean_obs = lax.fori_loop(0, members // 64, add_rows, jnp.zeros((1, obs), F32)) / members
    innovation = ((values - mean_obs) / errors).astype(BF)

    def scale_rows(i, _):
        at = pl.ds(pl.multiple_of(i * 64, 64), 64)
        anomaly = (raw[at, :].astype(F32) - mean_obs).astype(BF)
        scaled[at, :] = (anomaly.astype(F32) * inverse).astype(BF)
        return 0

    lax.fori_loop(0, members // 64, scale_rows, 0)
    spread16 = jnp.where(iota((16, obs), 0) == 0, innovation.astype(F32), 0.0).astype(BF)
    projected = jnp.sum(nt(spread16, scaled[...]), axis=0, keepdims=True)

    nb = members // LANES
    lane, line = iota((LANES, LANES), 1), iota((LANES, LANES), 0)
    place = 0
    for bi in range(nb):
        strip = nt(scaled[bi * LANES:(bi + 1) * LANES, :], scaled[bi * LANES:, :])
        for bj in range(bi, nb):
            blk = strip[:, (bj - bi) * LANES:(bj - bi + 1) * LANES]
            if bi == bj:
                chunk = projected[:, bi * LANES:(bi + 1) * LANES]
                turned = pltpu.roll(jnp.broadcast_to(chunk, (8, LANES)), LANES // 2, 1)[0:1, :]
                low = lane < LANES // 2
                blk = jnp.where(low & (line == LANES - 1), chunk, blk)
                blk = jnp.where(low & (line == LANES - 2), turned, blk)
            gram[place * LANES:(place + 1) * LANES, :] = blk
            place += 1
    if place * LANES < total:
        gram[place * LANES:, :] = jnp.zeros((total - place * LANES, LANES), F32)

    def cut(start, size):
        return pl.ds(pl.multiple_of(start, 8), size)

    go = remote(gram.at[cut((1 - core) * half, half)], r1, c_send, c_recv, {"mem": mate})
    go.start()
    go.wait_recv()
    s1[...] = gram[cut(core * half, half), :] + r1[...]

    def to_chip(d):
        return lax.rem(lax.rem(chip + d, nq) * 2 + core, n)

    def plane(d):
        q = lax.rem(chip + d, nq)
        return remote(s1.at[cut(q * quart, quart)], r2.at[d], q_send.at[d], q_recv.at[d], {"mem": to_chip(d)})

    for d in range(1, nq):
        plane(d).start()
    acc = s1[cut(chip * quart, quart), :]
    for d in range(1, nq):
        plane(d).wait_recv()
        acc = acc + r2[d]
    s2[...] = acc

    def block_copy(p, at):
        return remote(x.at[:, col(p)], held.at[block(at)], a_send.at[p], a_recv.at[at], {"mem": p})

    def take(p):
        got = held[block(p), :]
        for f in range(fields):
            pick = jnp.where(iota((mloc, rows), 1) == iota((mloc, rows), 0) * fields + f, 1.0, 0.0).astype(BF)
            lines = nn(pick, got)
            at = slice(f * cells, (f + 1) * cells)
            anom[share(p), at] = lines.astype(BF)
            means[:, at] += jnp.sum(lines, axis=0, keepdims=True)

    def send_block(j, _):
        block_copy(peer(j), me).start()
        return 0

    def get_block(j, _):
        p = source(j)
        block_copy(p, p).wait_recv()
        take(p)
        return 0

    def line_of(d):
        k = lax.rem(mz + d, nz)
        return remote(s2.at[cut(k * piece, piece)], r3.at[d], z_send.at[d], z_recv.at[d], {"cell": k})

    for d in range(1, nz):
        line_of(d).start()
    send_block(1, 0)
    own = pltpu.make_async_copy(x.at[:, col(me)], held.at[block(me)], own_sem)
    own.start()
    means[...] = jnp.zeros_like(means)
    own.wait()
    take(me)
    acc = s2[cut(mz * piece, piece), :]
    for d in range(1, nz):
        line_of(d).wait_recv()
        acc = acc + r3[d]
    mine = core * half + chip * quart
    full[cut(mine + mz * piece, piece), :] = acc

    def line_back(d, k):
        at = full.at[cut(mine + k * piece, piece)]
        return remote(at, at, zg_send.at[d], zg_recv.at[d], {"cell": lax.rem(mz + d, nz)})

    for d in range(1, nz):
        line_back(d, mz).start()
    get_block(1, 0)
    for d in range(1, nz):
        line_back(d, lax.rem(mz + nz - d, nz)).wait_recv()

    def plane_back(d, q):
        at = full.at[cut(core * half + q * quart, quart)]
        return remote(at, at, qg_send.at[d], qg_recv.at[d], {"mem": to_chip(d)})

    def pair_back(d, c, q):
        at = full.at[cut(c * half + q * quart, quart)]
        return remote(at, at, cg_send.at[d], cg_recv.at[d], {"mem": mate})

    for d in range(1, nq):
        plane_back(d, chip).start()
    pair_back(0, core, chip).start()
    for d in range(1, nq):
        q = lax.rem(chip + nq - d, nq)
        plane_back(d, q).wait_recv()
        pair_back(d, core, q).start()
    lax.fori_loop(2, n, send_block, 0)
    for d in range(nq):
        pair_back(d, 1 - core, lax.rem(chip + nq - d, nq)).wait_recv()

    place = 0
    squares = jnp.zeros((1, LANES), F32)
    proj = []
    for bi in range(nb):
        for bj in range(bi, nb):
            blk = full[place * LANES:(place + 1) * LANES, :]
            place += 1
            here, there = slice(bi * LANES, (bi + 1) * LANES), slice(bj * LANES, (bj + 1) * LANES)
            if bi == bj:
                first, second = blk[LANES - 1:, :], blk[LANES - 2:LANES - 1, :]
                second = pltpu.roll(jnp.broadcast_to(second, (8, LANES)), LANES // 2, 1)[0:1, :]
                proj.append(jnp.where(iota((1, LANES), 1) < LANES // 2, first, second))
                blk = jnp.where(lane >= line, blk, blk.T) + jnp.where(lane == line, 1.0, 0.0)
                sys_f[here, here] = blk
                squares = squares + jnp.sum(blk * blk, axis=0, keepdims=True)
            else:
                sys_f[here, there] = blk
                sys_f[there, here] = blk.T
                squares = squares + 2.0 * jnp.sum(blk * blk, axis=0, keepdims=True)
    projected = jnp.concatenate(proj, axis=1)
    norm_scale = jnp.sqrt(jnp.sum(squares, axis=1, keepdims=True))
    inv_norm = 1.0 / norm_scale

    IP, IU, IQ, IT, IZ = range(5)
    step = 256 if members % 256 == 0 else LANES
    chunks = members // step

    def keep(slot, at, val):
        hi = val.astype(BF)
        his[slot, at, :] = hi
        los[slot, at, :] = (val - hi.astype(F32)).astype(BF)

    def times(a, b, finish):
        right = jnp.concatenate([his[b], los[b], his[b]], axis=0)
        for i in range(chunks):
            at = slice(i * step, (i + 1) * step)
            ah, al = his[a, at, :], los[a, at, :]
            finish(at, i, nn(jnp.concatenate([ah, ah, al], axis=1), right))

    def scale(i, _):
        at = pl.ds(pl.multiple_of(i * 64, 64), 64)
        val = sys_f[at, :] * inv_norm
        sys_f[at, :] = val
        keep(IP, at, val)
        return 0

    lax.fori_loop(0, members // 64, scale, 0)

    def quartic(into):
        def first(at, i, val):
            val = val - 4.5 * sys_f[at, :]
            u_f[at, :] = val
            keep(IU, at, val)

        times(IP, IP, first)

        def second(at, i, val):
            val = 0.0625 * val + 0.421875 * u_f[at, :] - 0.5390625 * sys_f[at, :]
            diagonal = iota((step, members), 1) == iota((step, members), 0) + i * step
            val = val + jnp.where(diagonal, 2.25, 0.0)
            for slot in into:
                keep(slot, at, val)

        times(IU, IU, second)

    def renew():
        times(IQ, IP, lambda at, i, val: keep(IT, at, val))

        def last(at, i, val):
            sys_f[at, :] = val
            keep(IP, at, val)

        times(IQ, IT, last)

    quartic((IQ, IZ))
    renew()

    def pair_turn(turn, _):
        now = IZ + turn
        quartic((IQ,))
        times(IQ, now, lambda at, i, val: keep(now + 1, at, val))
        renew()
        return 0

    lax.fori_loop(0, NS_ITERS // 2 - 2, pair_turn, 0)
    quartic((IQ,))

    def final(at, i, val):
        z_f[at, :] = val

    times(IQ, IZ + NS_ITERS // 2 - 2, final)

    def get_two(i, _):
        p, q = source(2 * i), source(2 * i + 1)
        block_copy(p, p).wait_recv()
        block_copy(q, q).wait_recv()
        take(p)
        take(q)
        return 0

    lax.fori_loop(1, n // 2, get_two, 0)
    means[...] = means[...] / members

    def centre(i, _):
        at = pl.ds(pl.multiple_of(i * 64, 64), 64)
        anom[at, :] = (anom[at, :].astype(F32) - means[...]).astype(BF)
        return 0

    lax.fori_loop(0, members // 64, centre, 0)

    root = 1.0 / jnp.sqrt(norm_scale)

    def weigh(i, carry):
        at = pl.ds(pl.multiple_of(i * 64, 64), 64)
        val = z_f[at, :]
        w = (val * root).astype(BF)
        wts[at, :] = w
        shift = jnp.sum(val * projected, axis=1, keepdims=True) * (root * (1.0 / norm_factor))
        return carry + jnp.sum(shift * w.astype(F32), axis=0, keepdims=True)

    mixed = lax.fori_loop(0, members // 64, weigh, jnp.zeros((1, members), F32))
    line = iota((16, members), 0)
    stack = jnp.zeros((16, members), F32)
    for i, part in enumerate(thirds(mixed)):
        stack = jnp.where(line == i, part.astype(F32), stack)
    mix[...] = stack.astype(BF)

    def make(p):
        double = jnp.where(
            (iota((rows, mloc), 0) >= iota((rows, mloc), 1) * fields)
            & (iota((rows, mloc), 0) < iota((rows, mloc), 1) * fields + fields), 1.0, 0.0).astype(BF)
        w2 = jnp.concatenate([nn(double, wts[share(p), :]).astype(BF), mix[...]], axis=0)
        field = iota((rows, cells), 0) & (fields - 1)
        out = None
        for f in range(fields):
            at = slice(f * cells, (f + 1) * cells)
            part = nn(w2, anom[:, at])
            shift = jnp.sum(part[rows:, :], axis=0, keepdims=True)
            part = part[:rows, :] + (means[:, at] + shift)
            out = part if out is None else jnp.where(field == f, part, out)
        return out.astype(BF)

    def out_copy(p, at):
        return remote(outs.at[p], y.at[:, col(at)], o_send.at[p], o_recv.at[at], {"mem": p})

    def send_out(j, _):
        p = peer(j)
        outs[p] = make(p)
        out_copy(p, me).start()
        return 0

    lax.fori_loop(1, n, send_out, 0)
    outs[me] = make(me)
    own = pltpu.make_async_copy(outs.at[me], y.at[:, col(me)], own_sem)
    own.start()

    def finish_out(j, _):
        p = source(j)
        out_copy(p, p).wait_recv()
        return 0

    lax.fori_loop(1, n, finish_out, 0)
    own.wait()

    def sent(j, _):
        p = peer(j)
        place_copy(p, me).wait_send()
        pick_copy(p, me).wait_send()
        block_copy(p, me).wait_send()
        out_copy(p, me).wait_send()
        return 0

    lax.fori_loop(1, n, sent, 0)
    go.wait_send()
    for d in range(1, nq):
        plane(d).wait_send()
        plane_back(d, chip).wait_send()
    for d in range(1, nz):
        line_of(d).wait_send()
        line_back(d, mz).wait_send()
    for d in range(nq):
        pair_back(d, core, lax.rem(chip + nq - d, nq)).wait_send()


def local(prior_ensemble, measurement_location, measurement_datum, measurement_spread):
    n, nz = lax.axis_size("mem"), lax.axis_size("cell")
    mloc, fields, width = prior_ensemble.shape
    members, cells, rows = mloc * n, width // n, mloc * fields
    obs = measurement_location.size
    nb = members // LANES
    unit = 8 * n * nz
    total = -(-(nb * (nb + 1) // 2 * LANES) // unit) * unit
    half, nq = total // 2, n // 2
    quart = half // nq
    piece = quart // nz
    dims = (n, nz, members, fields, cells, mloc, width * nz)
    zslots = 4 + NS_ITERS // 2 - 1
    vm, dma = pltpu.VMEM, pltpu.SemaphoreType.DMA
    square = (members, members)
    scratch = [
        vm((rows, width), BF), vm((n,) + measurement_location.shape, jnp.int32),
        vm((n, mloc, obs), BF), vm((members, obs), BF),
        vm((n * rows, cells), BF), vm((members, fields * cells), BF), vm((1, fields * cells), F32),
        vm((members, obs), BF),
        vm((total, LANES), F32), vm((half, LANES), F32), vm((half, LANES), F32),
        vm((nq, quart, LANES), F32), vm((quart, LANES), F32), vm((nz, piece, LANES), F32),
        vm((total, LANES), F32),
        vm(square, F32), vm(square, F32), vm(square, F32),
        vm((zslots,) + square, BF), vm((zslots,) + square, BF), vm(square, BF),
        vm((16, members), BF), vm((n, rows, cells), BF),
        dma, dma((n,)), dma((n,)), dma((n,)), dma((n,)),
        dma((n,)), dma((n,)), dma, dma, dma, dma((nq,)), dma((nq,)), dma((nz,)), dma((nz,)),
        dma((nz,)), dma((nz,)), dma((nq,)), dma((nq,)), dma((nq,)), dma((nq,)), dma((n,)), dma((n,)),
    ]
    out = pl.pallas_call(
        functools.partial(kernel, dims),
        out_shape=jax.ShapeDtypeStruct((rows, width), BF),
        in_specs=[pl.BlockSpec(memory_space=pl.ANY)] + [pl.BlockSpec(memory_space=pltpu.VMEM)] * 3,
        out_specs=pl.BlockSpec(memory_space=pl.ANY),
        scratch_shapes=scratch,
        compiler_params=pltpu.CompilerParams(
            collective_id=0, has_side_effects=True, vmem_limit_bytes=50 * 1024 * 1024
        ),
    )(prior_ensemble.reshape(rows, width), measurement_location, measurement_datum, measurement_spread)
    return out.reshape(mloc, fields, width)


def solution(mesh):
    placed = (P("mem", None, "cell"), P("cell", "mem"), P("cell", "mem"), P("cell", "mem"))
    return jax.shard_map(
        local, mesh=mesh, in_specs=placed, out_specs=P("mem", None, "cell"), check_vma=False
    )
```

```python
import functools
import math

import jax
import jax.numpy as jnp
from jax import lax
from jax.experimental import pallas as pl
from jax.experimental.pallas import tpu as pltpu
from jax.sharding import PartitionSpec as P

NS_ITERS = 8
LANES = 128
BF, F32 = jnp.bfloat16, jnp.float32
MESH = pl.DeviceIdType.MESH


def iota(shape, dim):
    return lax.broadcasted_iota(jnp.int32, shape, dim)


def remote(src, dst, send, recv, where):
    return pltpu.make_async_remote_copy(
        src_ref=src, dst_ref=dst, send_sem=send, recv_sem=recv, device_id=where, device_id_type=MESH
    )


def nt(a, b):
    return lax.dot_general(a, b, (((1,), (1,)), ((), ())), preferred_element_type=F32)


def nn(a, b):
    return jnp.dot(a, b, preferred_element_type=F32)


def thirds(v):
    hi = v.astype(BF)
    rest = v - hi.astype(F32)
    mid = rest.astype(BF)
    lo = (rest - mid.astype(F32)).astype(BF)
    return hi, mid, lo


def kernel(
    dims, x, loc, datum, spread, y,
    near, places, picked, raw, held, anom, means, scaled, gram, r1, s1, r2, s2, r3, full,
    sys_f, u_f, z_f, his, los, wts, mix, outs,
    near_sem, l_send, l_recv, p_send, p_recv, a_send, a_recv, own_sem, c_send, c_recv, q_send, q_recv, z_send, z_recv,
    zg_send, zg_recv, qg_send, qg_recv, cg_send, cg_recv, o_send, o_recv,
):
    n, nz, members, fields, cells, mloc, grid_cells = dims
    rows = mloc * fields
    nq = n // 2
    total = gram.shape[0]
    half, quart = total // 2, total // 2 // nq
    piece = quart // nz
    norm_factor = math.sqrt(members - 1)
    me, mz = lax.axis_index("mem"), lax.axis_index("cell")
    core, chip = lax.rem(me, 2), lax.div(me, 2)
    mate = me + 1 - 2 * core

    fetch = pltpu.make_async_copy(x, near, near_sem)
    fetch.start()

    barrier = pltpu.get_barrier_semaphore()
    for d in range(1, n):
        pl.semaphore_signal(barrier, inc=1, device_id={"mem": lax.rem(me + d, n)}, device_id_type=MESH)
    for d in range(1, nz):
        pl.semaphore_signal(barrier, inc=1, device_id={"cell": lax.rem(mz + d, nz)}, device_id_type=MESH)
    pl.semaphore_wait(barrier, n - 1 + nz - 1)

    def col(p):
        return pl.ds(pl.multiple_of(p * cells, cells), cells)

    def block(p):
        return pl.ds(pl.multiple_of(p * rows, rows), rows)

    def share(p):
        return pl.ds(pl.multiple_of(p * mloc, mloc), mloc)

    def peer(j):
        return lax.rem(chip + lax.div(j, 2), nq) * 2 + lax.rem(core + j, 2)

    def source(j):
        return lax.rem(chip + nq - lax.div(j, 2), nq) * 2 + lax.rem(core + j, 2)

    def place_copy(p, at):
        return remote(loc, places.at[at], l_send.at[p], l_recv.at[at], {"mem": p})

    def send_places(j, _):
        place_copy(peer(j), me).start()
        return 0

    lax.fori_loop(1, n, send_places, 0)
    places[me] = loc[...]
    obs_rows = loc.shape[0]
    obs = obs_rows * LANES
    fetch.wait()

    def choose(p):
        v = places[p]
        field = jnp.zeros_like(v)
        for f in range(1, fields):
            field = field + jnp.where(v >= f * grid_cells, 1, 0)
        slots = v - field * grid_cells - (mz * n + p) * cells

        slot = jnp.concatenate([slots[r:r + 1, :] for r in range(obs_rows)], axis=1)
        hot = jnp.where(iota((cells, obs), 0) == slot, 1.0, 0.0).astype(BF)
        both = nn(near[:, col(p)], hot)
        wanted = jnp.concatenate([field[r:r + 1, :] for r in range(obs_rows)], axis=1)
        both = jnp.where((iota((rows, obs), 0) & (fields - 1)) == wanted, both, 0.0).astype(BF)
        low = iota((mloc, rows), 0) * fields
        join = jnp.where((iota((mloc, rows), 1) >= low) & (iota((mloc, rows), 1) < low + fields), 1.0, 0.0)
        return nn(join.astype(BF), both).astype(BF)

    def pick_copy(p, at):
        return remote(picked.at[p], raw.at[share(at)], p_send.at[p], p_recv.at[at], {"mem": p})

    def send_picked(i, _):
        p, q = peer(2 * i + 1), peer(2 * i + 2)
        place_copy(p, p).wait_recv()
        place_copy(q, q).wait_recv()
        first, second = choose(p), choose(q)
        picked[p] = first
        picked[q] = second
        pick_copy(p, me).start()
        pick_copy(q, me).start()
        return 0

    lax.fori_loop(0, n // 2 - 1, send_picked, 0)
    p = peer(n - 1)
    place_copy(p, p).wait_recv()
    first, second = choose(p), choose(me)
    picked[p] = first
    pick_copy(p, me).start()
    raw[share(me), :] = second

    def block_copy(p, at):
        return remote(x.at[:, col(p)], held.at[block(at)], a_send.at[p], a_recv.at[at], {"mem": p})

    def take(p):
        got = held[block(p), :]
        for f in range(fields):
            pick = jnp.where(iota((mloc, rows), 1) == iota((mloc, rows), 0) * fields + f, 1.0, 0.0).astype(BF)
            lines = nn(pick, got)
            at = slice(f * cells, (f + 1) * cells)
            anom[share(p), at] = lines.astype(BF)
            means[:, at] += jnp.sum(lines, axis=0, keepdims=True)

    def send_block(j, _):
        block_copy(peer(j), me).start()
        return 0

    def get_block(j, _):
        p = source(j)
        block_copy(p, p).wait_recv()
        take(p)
        return 0

    send_block(1, 0)
    send_block(2, 0)
    own = pltpu.make_async_copy(x.at[:, col(me)], held.at[block(me)], own_sem)
    own.start()
    means[...] = jnp.zeros_like(means)

    def get_picked(j, _):
        p = source(j)
        pick_copy(p, p).wait_recv()
        return 0

    lax.fori_loop(1, n, get_picked, 0)

    errors = jnp.concatenate([spread[r:r + 1, :] for r in range(obs_rows)], axis=1)
    values = jnp.concatenate([datum[r:r + 1, :] for r in range(obs_rows)], axis=1)
    inverse = 1.0 / (errors * norm_factor)

    def add_rows(i, carry):
        at = pl.ds(pl.multiple_of(i * 64, 64), 64)
        return carry + jnp.sum(raw[at, :].astype(F32), axis=0, keepdims=True)

    mean_obs = lax.fori_loop(0, members // 64, add_rows, jnp.zeros((1, obs), F32)) / members
    innovation = ((values - mean_obs) / errors).astype(BF)

    def scale_rows(i, _):
        at = pl.ds(pl.multiple_of(i * 64, 64), 64)
        anomaly = (raw[at, :].astype(F32) - mean_obs).astype(BF)
        scaled[at, :] = (anomaly.astype(F32) * inverse).astype(BF)
        return 0

    lax.fori_loop(0, members // 64, scale_rows, 0)
    spread16 = jnp.where(iota((16, obs), 0) == 0, innovation.astype(F32), 0.0).astype(BF)
    projected = jnp.sum(nt(spread16, scaled[...]), axis=0, keepdims=True)

    nb = members // LANES
    lane, line = iota((LANES, LANES), 1), iota((LANES, LANES), 0)
    place = 0
    for bi in range(nb):
        strip = nt(scaled[bi * LANES:(bi + 1) * LANES, :], scaled[bi * LANES:, :])
        for bj in range(bi, nb):
            blk = strip[:, (bj - bi) * LANES:(bj - bi + 1) * LANES]
            if bi == bj:
                chunk = projected[:, bi * LANES:(bi + 1) * LANES]
                turned = pltpu.roll(jnp.broadcast_to(chunk, (8, LANES)), LANES // 2, 1)[0:1, :]
                low = lane < LANES // 2
                blk = jnp.where(low & (line == LANES - 1), chunk, blk)
                blk = jnp.where(low & (line == LANES - 2), turned, blk)
            gram[place * LANES:(place + 1) * LANES, :] = blk
            place += 1
    if place * LANES < total:
        gram[place * LANES:, :] = jnp.zeros((total - place * LANES, LANES), F32)

    def cut(start, size):
        return pl.ds(pl.multiple_of(start, 8), size)

    go = remote(gram.at[cut((1 - core) * half, half)], r1, c_send, c_recv, {"mem": mate})
    go.start()
    own.wait()
    take(me)
    go.wait_recv()
    s1[...] = gram[cut(core * half, half), :] + r1[...]

    def to_chip(d):
        return lax.rem(lax.rem(chip + d, nq) * 2 + core, n)

    def plane(d):
        q = lax.rem(chip + d, nq)
        return remote(s1.at[cut(q * quart, quart)], r2.at[d], q_send.at[d], q_recv.at[d], {"mem": to_chip(d)})

    for d in range(1, nq):
        plane(d).start()
    get_block(1, 0)
    acc = s1[cut(chip * quart, quart), :]
    for d in range(1, nq):
        plane(d).wait_recv()
        acc = acc + r2[d]
    s2[...] = acc

    def line_of(d):
        k = lax.rem(mz + d, nz)
        return remote(s2.at[cut(k * piece, piece)], r3.at[d], z_send.at[d], z_recv.at[d], {"cell": k})

    for d in range(1, nz):
        line_of(d).start()
    send_block(3, 0)
    get_block(2, 0)
    acc = s2[cut(mz * piece, piece), :]
    for d in range(1, nz):
        line_of(d).wait_recv()
        acc = acc + r3[d]
    mine = core * half + chip * quart
    full[cut(mine + mz * piece, piece), :] = acc

    def line_back(d, k):
        at = full.at[cut(mine + k * piece, piece)]
        return remote(at, at, zg_send.at[d], zg_recv.at[d], {"cell": lax.rem(mz + d, nz)})

    for d in range(1, nz):
        line_back(d, mz).start()
    for d in range(1, nz):
        line_back(d, lax.rem(mz + nz - d, nz)).wait_recv()

    def plane_back(d, q):
        at = full.at[cut(core * half + q * quart, quart)]
        return remote(at, at, qg_send.at[d], qg_recv.at[d], {"mem": to_chip(d)})

    def pair_back(d, c, q):
        at = full.at[cut(c * half + q * quart, quart)]
        return remote(at, at, cg_send.at[d], cg_recv.at[d], {"mem": mate})

    for d in range(1, nq):
        plane_back(d, chip).start()
    pair_back(0, core, chip).start()
    get_block(3, 0)
    for d in range(1, nq):
        q = lax.rem(chip + nq - d, nq)
        plane_back(d, q).wait_recv()
        pair_back(d, core, q).start()
    lax.fori_loop(4, n, send_block, 0)
    for d in range(nq):
        pair_back(d, 1 - core, lax.rem(chip + nq - d, nq)).wait_recv()

    place = 0
    squares = jnp.zeros((1, LANES), F32)
    proj = []
    for bi in range(nb):
        for bj in range(bi, nb):
            blk = full[place * LANES:(place + 1) * LANES, :]
            place += 1
            here, there = slice(bi * LANES, (bi + 1) * LANES), slice(bj * LANES, (bj + 1) * LANES)
            if bi == bj:
                first, second = blk[LANES - 1:, :], blk[LANES - 2:LANES - 1, :]
                second = pltpu.roll(jnp.broadcast_to(second, (8, LANES)), LANES // 2, 1)[0:1, :]
                proj.append(jnp.where(iota((1, LANES), 1) < LANES // 2, first, second))
                blk = jnp.where(lane >= line, blk, blk.T) + jnp.where(lane == line, 1.0, 0.0)
                sys_f[here, here] = blk
                squares = squares + jnp.sum(blk * blk, axis=0, keepdims=True)
            else:
                sys_f[here, there] = blk
                sys_f[there, here] = blk.T
                squares = squares + 2.0 * jnp.sum(blk * blk, axis=0, keepdims=True)
    projected = jnp.concatenate(proj, axis=1)
    norm_scale = jnp.sqrt(jnp.sum(squares, axis=1, keepdims=True))
    inv_norm = 1.0 / norm_scale

    IP, IU, IQ, IT, IZ = range(5)
    step = 256 if members % 256 == 0 else LANES
    chunks = members // step

    def keep(slot, at, val):
        hi = val.astype(BF)
        his[slot, at, :] = hi
        los[slot, at, :] = (val - hi.astype(F32)).astype(BF)

    def times(a, b, finish):
        right = jnp.concatenate([his[b], los[b], his[b]], axis=0)
        for i in range(chunks):
            at = slice(i * step, (i + 1) * step)
            ah, al = his[a, at, :], los[a, at, :]
            finish(at, i, nn(jnp.concatenate([ah, ah, al], axis=1), right))

    def scale(i, _):
        at = pl.ds(pl.multiple_of(i * 64, 64), 64)
        val = sys_f[at, :] * inv_norm
        sys_f[at, :] = val
        keep(IP, at, val)
        return 0

    lax.fori_loop(0, members // 64, scale, 0)

    def quartic(into):
        def first(at, i, val):
            val = val - 4.5 * sys_f[at, :]
            u_f[at, :] = val
            keep(IU, at, val)

        times(IP, IP, first)

        def second(at, i, val):
            val = 0.0625 * val + 0.421875 * u_f[at, :] - 0.5390625 * sys_f[at, :]
            diagonal = iota((step, members), 1) == iota((step, members), 0) + i * step
            val = val + jnp.where(diagonal, 2.25, 0.0)
            for slot in into:
                keep(slot, at, val)

        times(IU, IU, second)

    def renew():
        times(IQ, IP, lambda at, i, val: keep(IT, at, val))

        def last(at, i, val):
            sys_f[at, :] = val
            keep(IP, at, val)

        times(IQ, IT, last)

    quartic((IQ, IZ))
    renew()

    def pair_turn(turn, _):
        now = IZ + turn
        quartic((IQ,))
        times(IQ, now, lambda at, i, val: keep(now + 1, at, val))
        renew()
        return 0

    lax.fori_loop(0, NS_ITERS // 2 - 2, pair_turn, 0)
    quartic((IQ,))

    def final(at, i, val):
        z_f[at, :] = val

    times(IQ, IZ + NS_ITERS // 2 - 2, final)

    def get_two(i, _):
        p, q = source(2 * i), source(2 * i + 1)
        block_copy(p, p).wait_recv()
        block_copy(q, q).wait_recv()
        take(p)
        take(q)
        return 0

    lax.fori_loop(2, n // 2, get_two, 0)
    means[...] = means[...] / members

    def centre(i, _):
        at = pl.ds(pl.multiple_of(i * 64, 64), 64)
        anom[at, :] = (anom[at, :].astype(F32) - means[...]).astype(BF)
        return 0

    lax.fori_loop(0, members // 64, centre, 0)

    root = 1.0 / jnp.sqrt(norm_scale)

    def weigh(i, carry):
        at = pl.ds(pl.multiple_of(i * 64, 64), 64)
        val = z_f[at, :]
        w = (val * root).astype(BF)
        wts[at, :] = w
        shift = jnp.sum(val * projected, axis=1, keepdims=True) * (root * (1.0 / norm_factor))
        return carry + jnp.sum(shift * w.astype(F32), axis=0, keepdims=True)

    mixed = lax.fori_loop(0, members // 64, weigh, jnp.zeros((1, members), F32))
    line = iota((16, members), 0)
    stack = jnp.zeros((16, members), F32)
    for i, part in enumerate(thirds(mixed)):
        stack = jnp.where(line == i, part.astype(F32), stack)
    mix[...] = stack.astype(BF)

    def make(p):
        double = jnp.where(
            (iota((rows, mloc), 0) >= iota((rows, mloc), 1) * fields)
            & (iota((rows, mloc), 0) < iota((rows, mloc), 1) * fields + fields), 1.0, 0.0).astype(BF)
        w2 = jnp.concatenate([nn(double, wts[share(p), :]).astype(BF), mix[...]], axis=0)
        field = iota((rows, cells), 0) & (fields - 1)
        out = None
        for f in range(fields):
            at = slice(f * cells, (f + 1) * cells)
            part = nn(w2, anom[:, at])
            shift = jnp.sum(part[rows:, :], axis=0, keepdims=True)
            part = part[:rows, :] + (means[:, at] + shift)
            out = part if out is None else jnp.where(field == f, part, out)
        return out.astype(BF)

    def out_copy(p, at):
        return remote(outs.at[p], y.at[:, col(at)], o_send.at[p], o_recv.at[at], {"mem": p})

    def send_out(j, _):
        p = peer(j)
        outs[p] = make(p)
        out_copy(p, me).start()
        return 0

    lax.fori_loop(1, n, send_out, 0)
    outs[me] = make(me)
    own = pltpu.make_async_copy(outs.at[me], y.at[:, col(me)], own_sem)
    own.start()

    def finish_out(j, _):
        p = source(j)
        out_copy(p, p).wait_recv()
        return 0

    lax.fori_loop(1, n, finish_out, 0)
    own.wait()

    def sent(j, _):
        p = peer(j)
        place_copy(p, me).wait_send()
        pick_copy(p, me).wait_send()
        block_copy(p, me).wait_send()
        out_copy(p, me).wait_send()
        return 0

    lax.fori_loop(1, n, sent, 0)
    go.wait_send()
    for d in range(1, nq):
        plane(d).wait_send()
        plane_back(d, chip).wait_send()
    for d in range(1, nz):
        line_of(d).wait_send()
        line_back(d, mz).wait_send()
    for d in range(nq):
        pair_back(d, core, lax.rem(chip + nq - d, nq)).wait_send()


def local(prior_ensemble, measurement_location, measurement_datum, measurement_spread):
    n, nz = lax.axis_size("mem"), lax.axis_size("cell")
    mloc, fields, width = prior_ensemble.shape
    members, cells, rows = mloc * n, width // n, mloc * fields
    obs = measurement_location.size
    nb = members // LANES
    unit = 8 * n * nz
    total = -(-(nb * (nb + 1) // 2 * LANES) // unit) * unit
    half, nq = total // 2, n // 2
    quart = half // nq
    piece = quart // nz
    dims = (n, nz, members, fields, cells, mloc, width * nz)
    zslots = 4 + NS_ITERS // 2 - 1
    vm, dma = pltpu.VMEM, pltpu.SemaphoreType.DMA
    square = (members, members)
    scratch = [
        vm((rows, width), BF), vm((n,) + measurement_location.shape, jnp.int32),
        vm((n, mloc, obs), BF), vm((members, obs), BF),
        vm((n * rows, cells), BF), vm((members, fields * cells), BF), vm((1, fields * cells), F32),
        vm((members, obs), BF),
        vm((total, LANES), F32), vm((half, LANES), F32), vm((half, LANES), F32),
        vm((nq, quart, LANES), F32), vm((quart, LANES), F32), vm((nz, piece, LANES), F32),
        vm((total, LANES), F32),
        vm(square, F32), vm(square, F32), vm(square, F32),
        vm((zslots,) + square, BF), vm((zslots,) + square, BF), vm(square, BF),
        vm((16, members), BF), vm((n, rows, cells), BF),
        dma, dma((n,)), dma((n,)), dma((n,)), dma((n,)),
        dma((n,)), dma((n,)), dma, dma, dma, dma((nq,)), dma((nq,)), dma((nz,)), dma((nz,)),
        dma((nz,)), dma((nz,)), dma((nq,)), dma((nq,)), dma((nq,)), dma((nq,)), dma((n,)), dma((n,)),
    ]
    out = pl.pallas_call(
        functools.partial(kernel, dims),
        out_shape=jax.ShapeDtypeStruct((rows, width), BF),
        in_specs=[pl.BlockSpec(memory_space=pl.ANY)] + [pl.BlockSpec(memory_space=pltpu.VMEM)] * 3,
        out_specs=pl.BlockSpec(memory_space=pl.ANY),
        scratch_shapes=scratch,
        compiler_params=pltpu.CompilerParams(
            collective_id=0, has_side_effects=True, vmem_limit_bytes=50 * 1024 * 1024
        ),
    )(prior_ensemble.reshape(rows, width), measurement_location, measurement_datum, measurement_spread)
    return out.reshape(mloc, fields, width)


def solution(mesh):
    placed = (P("mem", None, "cell"), P("cell", "mem"), P("cell", "mem"), P("cell", "mem"))
    return jax.shard_map(
        local, mesh=mesh, in_specs=placed, out_specs=P("mem", None, "cell"), check_vma=False
    )
```

```python
import functools
import math

import jax
import jax.numpy as jnp
from jax import lax
from jax.experimental import pallas as pl
from jax.experimental.pallas import tpu as pltpu
from jax.sharding import PartitionSpec as P

NS_ITERS = 8
LANES = 128
BF, F32 = jnp.bfloat16, jnp.float32
MESH = pl.DeviceIdType.MESH


def iota(shape, dim):
    return lax.broadcasted_iota(jnp.int32, shape, dim)


def remote(src, dst, send, recv, where):
    return pltpu.make_async_remote_copy(
        src_ref=src, dst_ref=dst, send_sem=send, recv_sem=recv, device_id=where, device_id_type=MESH
    )


def nt(a, b):
    return lax.dot_general(a, b, (((1,), (1,)), ((), ())), preferred_element_type=F32)


def nn(a, b):
    return jnp.dot(a, b, preferred_element_type=F32)


def thirds(v):
    hi = v.astype(BF)
    rest = v - hi.astype(F32)
    mid = rest.astype(BF)
    lo = (rest - mid.astype(F32)).astype(BF)
    return hi, mid, lo


def kernel(
    dims, x, loc, datum, spread, y,
    near, places, picked, raw, held, anom, means, scaled, gram, r1, s1, r2, s2, r3, full,
    sys_f, u_f, z_f, his, los, wts, mix, outs,
    near_sem, l_send, l_recv, p_send, p_recv, a_send, a_recv, own_sem, c_send, c_recv, q_send, q_recv, z_send, z_recv,
    zg_send, zg_recv, qg_send, qg_recv, cg_send, cg_recv, o_send, o_recv,
):
    n, nz, members, fields, cells, mloc, grid_cells = dims
    rows = mloc * fields
    nq = n // 2
    total = gram.shape[0]
    half, quart = total // 2, total // 2 // nq
    piece = quart // nz
    norm_factor = math.sqrt(members - 1)
    me, mz = lax.axis_index("mem"), lax.axis_index("cell")
    core, chip = lax.rem(me, 2), lax.div(me, 2)
    mate = me + 1 - 2 * core

    fetch = pltpu.make_async_copy(x, near, near_sem)
    fetch.start()

    barrier = pltpu.get_barrier_semaphore()
    for d in range(1, n):
        pl.semaphore_signal(barrier, inc=1, device_id={"mem": lax.rem(me + d, n)}, device_id_type=MESH)
    for d in range(1, nz):
        pl.semaphore_signal(barrier, inc=1, device_id={"cell": lax.rem(mz + d, nz)}, device_id_type=MESH)
    pl.semaphore_wait(barrier, n - 1 + nz - 1)

    def col(p):
        return pl.ds(pl.multiple_of(p * cells, cells), cells)

    def block(p):
        return pl.ds(pl.multiple_of(p * rows, rows), rows)

    def share(p):
        return pl.ds(pl.multiple_of(p * mloc, mloc), mloc)

    def peer(j):
        return lax.rem(chip + lax.div(j, 2), nq) * 2 + lax.rem(core + j, 2)

    def source(j):
        return lax.rem(chip + nq - lax.div(j, 2), nq) * 2 + lax.rem(core + j, 2)

    def place_copy(p, at):
        return remote(loc, places.at[at], l_send.at[p], l_recv.at[at], {"mem": p})

    def send_places(j, _):
        place_copy(peer(j), me).start()
        return 0

    lax.fori_loop(1, n, send_places, 0)
    places[me] = loc[...]
    obs_rows = loc.shape[0]
    obs = obs_rows * LANES
    fetch.wait()

    def choose(p):
        v = places[p]
        field = jnp.zeros_like(v)
        for f in range(1, fields):
            field = field + jnp.where(v >= f * grid_cells, 1, 0)
        slots = v - field * grid_cells - (mz * n + p) * cells

        slot = jnp.concatenate([slots[r:r + 1, :] for r in range(obs_rows)], axis=1)
        hot = jnp.where(iota((cells, obs), 0) == slot, 1.0, 0.0).astype(BF)
        both = nn(near[:, col(p)], hot)
        wanted = jnp.concatenate([field[r:r + 1, :] for r in range(obs_rows)], axis=1)
        both = jnp.where((iota((rows, obs), 0) & (fields - 1)) == wanted, both, 0.0).astype(BF)
        low = iota((mloc, rows), 0) * fields
        join = jnp.where((iota((mloc, rows), 1) >= low) & (iota((mloc, rows), 1) < low + fields), 1.0, 0.0)
        return nn(join.astype(BF), both).astype(BF)

    def pick_copy(p, at):
        return remote(picked.at[p], raw.at[share(at)], p_send.at[p], p_recv.at[at], {"mem": p})

    def send_picked(i, _):
        p, q = peer(2 * i + 1), peer(2 * i + 2)
        place_copy(p, p).wait_recv()
        place_copy(q, q).wait_recv()
        first, second = choose(p), choose(q)
        picked[p] = first
        picked[q] = second
        pick_copy(p, me).start()
        pick_copy(q, me).start()
        return 0

    lax.fori_loop(0, n // 2 - 1, send_picked, 0)
    p = peer(n - 1)
    place_copy(p, p).wait_recv()
    first, second = choose(p), choose(me)
    picked[p] = first
    pick_copy(p, me).start()
    raw[share(me), :] = second

    def block_copy(p, at):
        return remote(x.at[:, col(p)], held.at[block(at)], a_send.at[p], a_recv.at[at], {"mem": p})

    def take(p):
        got = held[block(p), :]
        for f in range(fields):
            pick = jnp.where(iota((mloc, rows), 1) == iota((mloc, rows), 0) * fields + f, 1.0, 0.0).astype(BF)
            lines = nn(pick, got)
            at = slice(f * cells, (f + 1) * cells)
            anom[share(p), at] = lines.astype(BF)
            means[:, at] += jnp.sum(lines, axis=0, keepdims=True)

    def send_block(j, _):
        block_copy(peer(j), me).start()
        return 0

    def get_block(j, _):
        p = source(j)
        block_copy(p, p).wait_recv()
        take(p)
        return 0

    send_block(1, 0)
    send_block(2, 0)
    own = pltpu.make_async_copy(x.at[:, col(me)], held.at[block(me)], own_sem)
    own.start()
    means[...] = jnp.zeros_like(means)

    def get_picked(j, _):
        p = source(j)
        pick_copy(p, p).wait_recv()
        return 0

    lax.fori_loop(1, n, get_picked, 0)

    errors = jnp.concatenate([spread[r:r + 1, :] for r in range(obs_rows)], axis=1)
    values = jnp.concatenate([datum[r:r + 1, :] for r in range(obs_rows)], axis=1)
    inverse = 1.0 / (errors * norm_factor)

    def add_rows(i, carry):
        at = pl.ds(pl.multiple_of(i * 64, 64), 64)
        return carry + jnp.sum(raw[at, :].astype(F32), axis=0, keepdims=True)

    mean_obs = lax.fori_loop(0, members // 64, add_rows, jnp.zeros((1, obs), F32)) / members
    innovation = ((values - mean_obs) / errors).astype(BF)

    def scale_rows(i, _):
        at = pl.ds(pl.multiple_of(i * 64, 64), 64)
        anomaly = (raw[at, :].astype(F32) - mean_obs).astype(BF)
        scaled[at, :] = (anomaly.astype(F32) * inverse).astype(BF)
        return 0

    lax.fori_loop(0, members // 64, scale_rows, 0)
    spread16 = jnp.where(iota((16, obs), 0) == 0, innovation.astype(F32), 0.0).astype(BF)
    projected = jnp.sum(nt(spread16, scaled[...]), axis=0, keepdims=True)

    nb = members // LANES
    lane, line = iota((LANES, LANES), 1), iota((LANES, LANES), 0)
    place = 0
    for bi in range(nb):
        strip = nt(scaled[bi * LANES:(bi + 1) * LANES, :], scaled[bi * LANES:, :])
        for bj in range(bi, nb):
            blk = strip[:, (bj - bi) * LANES:(bj - bi + 1) * LANES]
            if bi == bj:
                chunk = projected[:, bi * LANES:(bi + 1) * LANES]
                turned = pltpu.roll(jnp.broadcast_to(chunk, (8, LANES)), LANES // 2, 1)[0:1, :]
                low = lane < LANES // 2
                blk = jnp.where(low & (line == LANES - 1), chunk, blk)
                blk = jnp.where(low & (line == LANES - 2), turned, blk)
            gram[place * LANES:(place + 1) * LANES, :] = blk
            place += 1
    if place * LANES < total:
        gram[place * LANES:, :] = jnp.zeros((total - place * LANES, LANES), F32)

    def cut(start, size):
        return pl.ds(pl.multiple_of(start, 8), size)

    go = remote(gram.at[cut((1 - core) * half, half)], r1, c_send, c_recv, {"mem": mate})
    go.start()
    own.wait()
    take(me)
    go.wait_recv()
    s1[...] = gram[cut(core * half, half), :] + r1[...]

    def to_chip(d):
        return lax.rem(lax.rem(chip + d, nq) * 2 + core, n)

    def plane(d):
        q = lax.rem(chip + d, nq)
        return remote(s1.at[cut(q * quart, quart)], r2.at[d], q_send.at[d], q_recv.at[d], {"mem": to_chip(d)})

    for d in range(1, nq):
        plane(d).start()
    get_block(1, 0)
    acc = s1[cut(chip * quart, quart), :]
    for d in range(1, nq):
        plane(d).wait_recv()
        acc = acc + r2[d]
    s2[...] = acc

    def line_of(d):
        k = lax.rem(mz + d, nz)
        return remote(s2.at[cut(k * piece, piece)], r3.at[d], z_send.at[d], z_recv.at[d], {"cell": k})

    for d in range(1, nz):
        line_of(d).start()
    send_block(3, 0)
    get_block(2, 0)
    acc = s2[cut(mz * piece, piece), :]
    for d in range(1, nz):
        line_of(d).wait_recv()
        acc = acc + r3[d]
    mine = core * half + chip * quart
    full[cut(mine + mz * piece, piece), :] = acc

    def line_back(d, k):
        at = full.at[cut(mine + k * piece, piece)]
        return remote(at, at, zg_send.at[d], zg_recv.at[d], {"cell": lax.rem(mz + d, nz)})

    for d in range(1, nz):
        line_back(d, mz).start()
    for d in range(1, nz):
        line_back(d, lax.rem(mz + nz - d, nz)).wait_recv()

    def plane_back(d, q):
        at = full.at[cut(core * half + q * quart, quart)]
        return remote(at, at, qg_send.at[d], qg_recv.at[d], {"mem": to_chip(d)})

    def pair_back(d, c, q):
        at = full.at[cut(c * half + q * quart, quart)]
        return remote(at, at, cg_send.at[d], cg_recv.at[d], {"mem": mate})

    for d in range(1, nq):
        plane_back(d, chip).start()
    pair_back(0, core, chip).start()
    get_block(3, 0)
    for d in range(1, nq):
        q = lax.rem(chip + nq - d, nq)
        plane_back(d, q).wait_recv()
        pair_back(d, core, q).start()
    lax.fori_loop(4, n, send_block, 0)
    for d in range(nq):
        pair_back(d, 1 - core, lax.rem(chip + nq - d, nq)).wait_recv()

    place = 0
    squares = jnp.zeros((1, LANES), F32)
    proj = []
    for bi in range(nb):
        for bj in range(bi, nb):
            blk = full[place * LANES:(place + 1) * LANES, :]
            place += 1
            here, there = slice(bi * LANES, (bi + 1) * LANES), slice(bj * LANES, (bj + 1) * LANES)
            if bi == bj:
                first, second = blk[LANES - 1:, :], blk[LANES - 2:LANES - 1, :]
                second = pltpu.roll(jnp.broadcast_to(second, (8, LANES)), LANES // 2, 1)[0:1, :]
                proj.append(jnp.where(iota((1, LANES), 1) < LANES // 2, first, second))
                blk = jnp.where(lane >= line, blk, blk.T) + jnp.where(lane == line, 1.0, 0.0)
                sys_f[here, here] = blk
                squares = squares + jnp.sum(blk * blk, axis=0, keepdims=True)
            else:
                sys_f[here, there] = blk
                sys_f[there, here] = blk.T
                squares = squares + 2.0 * jnp.sum(blk * blk, axis=0, keepdims=True)
    projected = jnp.concatenate(proj, axis=1)
    norm_scale = jnp.sqrt(jnp.sum(squares, axis=1, keepdims=True))
    inv_norm = 1.0 / norm_scale

    IP, IU, IQ, IT, IZ = range(5)
    step = members
    chunks = members // step

    def keep(slot, at, val):
        hi = val.astype(BF)
        his[slot, at, :] = hi
        los[slot, at, :] = (val - hi.astype(F32)).astype(BF)

    def times(a, b, finish):
        right = jnp.concatenate([his[b], los[b], his[b]], axis=0)
        for i in range(chunks):
            at = slice(i * step, (i + 1) * step)
            ah, al = his[a, at, :], los[a, at, :]
            finish(at, i, nn(jnp.concatenate([ah, ah, al], axis=1), right))

    def scale(i, _):
        at = pl.ds(pl.multiple_of(i * 64, 64), 64)
        val = sys_f[at, :] * inv_norm
        sys_f[at, :] = val
        keep(IP, at, val)
        return 0

    lax.fori_loop(0, members // 64, scale, 0)

    def quartic(into):
        def first(at, i, val):
            val = val - 4.5 * sys_f[at, :]
            u_f[at, :] = val
            keep(IU, at, val)

        times(IP, IP, first)

        def second(at, i, val):
            val = 0.0625 * val + 0.421875 * u_f[at, :] - 0.5390625 * sys_f[at, :]
            diagonal = iota((step, members), 1) == iota((step, members), 0) + i * step
            val = val + jnp.where(diagonal, 2.25, 0.0)
            for slot in into:
                keep(slot, at, val)

        times(IU, IU, second)

    def renew():
        times(IQ, IP, lambda at, i, val: keep(IT, at, val))

        def last(at, i, val):
            sys_f[at, :] = val
            keep(IP, at, val)

        times(IQ, IT, last)

    quartic((IQ, IZ))
    renew()

    def pair_turn(turn, _):
        now = IZ + turn
        quartic((IQ,))
        times(IQ, now, lambda at, i, val: keep(now + 1, at, val))
        renew()
        return 0

    lax.fori_loop(0, NS_ITERS // 2 - 2, pair_turn, 0)
    quartic((IQ,))

    def final(at, i, val):
        z_f[at, :] = val

    times(IQ, IZ + NS_ITERS // 2 - 2, final)

    def get_two(i, _):
        p, q = source(2 * i), source(2 * i + 1)
        block_copy(p, p).wait_recv()
        block_copy(q, q).wait_recv()
        take(p)
        take(q)
        return 0

    lax.fori_loop(2, n // 2, get_two, 0)
    means[...] = means[...] / members

    def centre(i, _):
        at = pl.ds(pl.multiple_of(i * 64, 64), 64)
        anom[at, :] = (anom[at, :].astype(F32) - means[...]).astype(BF)
        return 0

    lax.fori_loop(0, members // 64, centre, 0)

    root = 1.0 / jnp.sqrt(norm_scale)

    def weigh(i, carry):
        at = pl.ds(pl.multiple_of(i * 64, 64), 64)
        val = z_f[at, :]
        w = (val * root).astype(BF)
        wts[at, :] = w
        shift = jnp.sum(val * projected, axis=1, keepdims=True) * (root * (1.0 / norm_factor))
        return carry + jnp.sum(shift * w.astype(F32), axis=0, keepdims=True)

    mixed = lax.fori_loop(0, members // 64, weigh, jnp.zeros((1, members), F32))
    line = iota((16, members), 0)
    stack = jnp.zeros((16, members), F32)
    for i, part in enumerate(thirds(mixed)):
        stack = jnp.where(line == i, part.astype(F32), stack)
    mix[...] = stack.astype(BF)

    def make(p):
        double = jnp.where(
            (iota((rows, mloc), 0) >= iota((rows, mloc), 1) * fields)
            & (iota((rows, mloc), 0) < iota((rows, mloc), 1) * fields + fields), 1.0, 0.0).astype(BF)
        w2 = jnp.concatenate([nn(double, wts[share(p), :]).astype(BF), mix[...]], axis=0)
        field = iota((rows, cells), 0) & (fields - 1)
        out = None
        for f in range(fields):
            at = slice(f * cells, (f + 1) * cells)
            part = nn(w2, anom[:, at])
            shift = jnp.sum(part[rows:, :], axis=0, keepdims=True)
            part = part[:rows, :] + (means[:, at] + shift)
            out = part if out is None else jnp.where(field == f, part, out)
        return out.astype(BF)

    def out_copy(p, at):
        return remote(outs.at[p], y.at[:, col(at)], o_send.at[p], o_recv.at[at], {"mem": p})

    def send_out(i, _):
        turn = lax.div(i, nq - 1)
        p = peer(2 * (i - turn * (nq - 1) + 1) + turn)
        outs[p] = make(p)
        out_copy(p, me).start()
        return 0

    lax.fori_loop(0, n - 2, send_out, 0)
    outs[mate] = make(mate)
    out_copy(mate, me).start()
    outs[me] = make(me)
    own = pltpu.make_async_copy(outs.at[me], y.at[:, col(me)], own_sem)
    own.start()

    def finish_out(j, _):
        p = source(j)
        out_copy(p, p).wait_recv()
        return 0

    lax.fori_loop(1, n, finish_out, 0)
    own.wait()

    def sent(j, _):
        p = peer(j)
        place_copy(p, me).wait_send()
        pick_copy(p, me).wait_send()
        block_copy(p, me).wait_send()
        out_copy(p, me).wait_send()
        return 0

    lax.fori_loop(1, n, sent, 0)
    go.wait_send()
    for d in range(1, nq):
        plane(d).wait_send()
        plane_back(d, chip).wait_send()
    for d in range(1, nz):
        line_of(d).wait_send()
        line_back(d, mz).wait_send()
    for d in range(nq):
        pair_back(d, core, lax.rem(chip + nq - d, nq)).wait_send()


def local(prior_ensemble, measurement_location, measurement_datum, measurement_spread):
    n, nz = lax.axis_size("mem"), lax.axis_size("cell")
    mloc, fields, width = prior_ensemble.shape
    members, cells, rows = mloc * n, width // n, mloc * fields
    obs = measurement_location.size
    nb = members // LANES
    unit = 8 * n * nz
    total = -(-(nb * (nb + 1) // 2 * LANES) // unit) * unit
    half, nq = total // 2, n // 2
    quart = half // nq
    piece = quart // nz
    dims = (n, nz, members, fields, cells, mloc, width * nz)
    zslots = 4 + NS_ITERS // 2 - 1
    vm, dma = pltpu.VMEM, pltpu.SemaphoreType.DMA
    square = (members, members)
    scratch = [
        vm((rows, width), BF), vm((n,) + measurement_location.shape, jnp.int32),
        vm((n, mloc, obs), BF), vm((members, obs), BF),
        vm((n * rows, cells), BF), vm((members, fields * cells), BF), vm((1, fields * cells), F32),
        vm((members, obs), BF),
        vm((total, LANES), F32), vm((half, LANES), F32), vm((half, LANES), F32),
        vm((nq, quart, LANES), F32), vm((quart, LANES), F32), vm((nz, piece, LANES), F32),
        vm((total, LANES), F32),
        vm(square, F32), vm(square, F32), vm(square, F32),
        vm((zslots,) + square, BF), vm((zslots,) + square, BF), vm(square, BF),
        vm((16, members), BF), vm((n, rows, cells), BF),
        dma, dma((n,)), dma((n,)), dma((n,)), dma((n,)),
        dma((n,)), dma((n,)), dma, dma, dma, dma((nq,)), dma((nq,)), dma((nz,)), dma((nz,)),
        dma((nz,)), dma((nz,)), dma((nq,)), dma((nq,)), dma((nq,)), dma((nq,)), dma((n,)), dma((n,)),
    ]
    out = pl.pallas_call(
        functools.partial(kernel, dims),
        out_shape=jax.ShapeDtypeStruct((rows, width), BF),
        in_specs=[pl.BlockSpec(memory_space=pl.ANY)] + [pl.BlockSpec(memory_space=pltpu.VMEM)] * 3,
        out_specs=pl.BlockSpec(memory_space=pl.ANY),
        scratch_shapes=scratch,
        compiler_params=pltpu.CompilerParams(
            collective_id=0, has_side_effects=True, vmem_limit_bytes=50 * 1024 * 1024
        ),
    )(prior_ensemble.reshape(rows, width), measurement_location, measurement_datum, measurement_spread)
    return out.reshape(mloc, fields, width)


def solution(mesh):
    placed = (P("mem", None, "cell"), P("cell", "mem"), P("cell", "mem"), P("cell", "mem"))
    return jax.shard_map(
        local, mesh=mesh, in_specs=placed, out_specs=P("mem", None, "cell"), check_vma=False
    )
```
